32 devices in a mesh: seq: 8 (over z, x), head: 4 (over y, core).
Axes of the slice: x: 2, y: 2, z: 4, core: 2. Of those that a mesh axis runs over, the one named last changes fastest.
Arguments:
- att_query: bfloat16 [2048, 8, 128], P('seq', 'head'), may hold values from -9 to 9
- att_key: bfloat16 [2048, 8, 128], P('seq', 'head'), may hold values from -9 to 9
- att_value: bfloat16 [2048, 8, 128], P('seq', 'head'), may hold values from -6 to 6
- norm_gain: float32 [8, 128], P('head'), may hold values from 0.1 to 1.9
- dn_query: bfloat16 [2048, 8, 128], P('seq', 'head'), may hold values from -6 to 6
- dn_key: bfloat16 [2048, 8, 128], P('seq', 'head'), may hold values from -4 to 4
- write_rate: float32 [2048, 8], P('seq', 'head'), may hold values from 0.04 to 0.9
- log_decay: float32 [2048, 8], P('seq', 'head'), may hold values from -1 to 0
- out_grad: bfloat16 [2048, 8, 128], P('seq', 'head'), may hold values from -6 to 6
Outputs:
- block_out: bfloat16 [2048, 8, 128], P('seq', 'head')
- att_query_grad: bfloat16 [2048, 8, 128], P('seq', 'head')
- att_key_grad: bfloat16 [2048, 8, 128], P('seq', 'head')
- att_value_grad: bfloat16 [2048, 8, 128], P('seq', 'head')
- gain_grad: float32 [8, 128], P('head')
- dn_query_grad: bfloat16 [2048, 8, 128], P('seq', 'head')
- dn_key_grad: bfloat16 [2048, 8, 128], P('seq', 'head')
- rate_grad: float32 [2048, 8], P('seq', 'head')
- decay_grad: float32 [2048, 8], P('seq', 'head')
The draws below stay inside these ranges and needn't reach their ends.
All inputs are finite; a program needn't handle non-finite values.
Results may differ from the reference program's by a relative error of at most 0.018.
Values may be sent and summed in bfloat16 or wider, within the bound.
A program may use at most 64 MiB of HBM per device.

```python
import math
import jax
import jax.numpy as jnp
from jax import lax

TOK_DEV = 256
WIN = 1024
CH = 64
DH = 128
HEAD_TOTAL = 8
SEQUENCE_TOKENS = 2048


def base_field(key):
    return jnp.clip(jax.random.normal(key, (SEQUENCE_TOKENS, HEAD_TOTAL, DH), jnp.float32), -4.0, 4.0)


def draw_att_query(key, part):
    field = base_field(jax.random.fold_in(key, 21))
    return field.astype(jnp.bfloat16)


def draw_att_key(key, part):
    field = base_field(jax.random.fold_in(key, 22))
    return field.astype(jnp.bfloat16)


def draw_dn_key(key, part):
    key_pair = jax.random.split(jax.random.fold_in(key, 41), 2)
    shard_total = SEQUENCE_TOKENS // TOK_DEV
    chosen_count = max(4, DH // 8)
    scores = jax.random.randint(key_pair[0], (shard_total, HEAD_TOTAL, DH), 0, 1048576) * DH + jnp.arange(DH, dtype=jnp.int32)
    cutoff = lax.top_k(scores, chosen_count)[0][..., -1:]
    chosen = jnp.repeat(scores >= cutoff, TOK_DEV, axis=0)
    field = base_field(key_pair[1])
    return (field * jnp.where(chosen, 1.0, 0.03)).astype(jnp.bfloat16)


def draw_write_rate(key, part):
    key_pair = jax.random.split(jax.random.fold_in(key, 51), 2)
    head_base = jnp.exp(jax.random.uniform(key_pair[0], (HEAD_TOTAL,), jnp.float32, math.log(0.08), math.log(0.6)))
    jitter = jax.random.uniform(key_pair[1], (SEQUENCE_TOKENS, HEAD_TOTAL), jnp.float32, 0.5, 1.5)
    return jnp.minimum(head_base[None, :] * jitter, 0.9)


def draw_log_decay(key, part):
    split_random_keys = jax.random.split(jax.random.fold_in(key, 31), 7)
    quick_share = 0.5
    quick = jax.random.uniform(split_random_keys[0], (HEAD_TOTAL,), jnp.float32) < quick_share
    quick_rate = jax.random.uniform(split_random_keys[1], (HEAD_TOTAL,), jnp.float32, 1.0 / 50.0, 1.0 / 30.0)
    slow_rate = jax.random.uniform(split_random_keys[2], (HEAD_TOTAL,), jnp.float32, 0.1, 0.3) / SEQUENCE_TOKENS
    base_rate = jnp.where(quick, quick_rate, slow_rate)
    shard_factor = jnp.exp(jax.random.uniform(split_random_keys[3], (SEQUENCE_TOKENS // TOK_DEV, HEAD_TOTAL), jnp.float32, 0.0, 0.9))
    factor = jnp.repeat(shard_factor, TOK_DEV, axis=0)
    jitter = jax.random.uniform(split_random_keys[4], (SEQUENCE_TOKENS, HEAD_TOTAL), jnp.float32, 0.5, 1.5)
    spike_positions = jax.random.randint(split_random_keys[5], (1, HEAD_TOTAL, 3), 0, SEQUENCE_TOKENS)
    erased_values = jnp.any(jnp.arange(SEQUENCE_TOKENS)[:, None, None] == spike_positions, axis=2)
    drop = jnp.log(jax.random.uniform(split_random_keys[6], (SEQUENCE_TOKENS, HEAD_TOTAL), jnp.float32, 0.6, 0.85))
    return -base_rate[None, :] * factor * jitter + jnp.where(erased_values, drop, 0.0)


def shard_levels(rng, dims, cuts, low, top_value):
    def one(axis_at, blocks):
        steps = jax.random.uniform(jax.random.fold_in(jax.random.fold_in(rng, 6), axis_at), (blocks,), jnp.float32, low / len(cuts), top_value / len(cuts))
        return jnp.repeat(jnp.exp(steps), dims[axis_at] // blocks).reshape((-1,) + (1,) * (len(dims) - axis_at - 1))

    loudness = one(*cuts[0])
    for cut in cuts[1:]:
        loudness = loudness * one(*cut)
    return loudness


def gaussian(rng, extent, scale, bound, shards=(), kind=jnp.bfloat16):
    drawn = scale * jax.random.normal(rng, extent, jnp.float32)
    if shards:
        drawn = drawn * shard_levels(rng, extent, shards, -0.22, 0.18)
    return jnp.clip(drawn, -bound, bound).astype(kind)


def setup_inputs(seed: int = 0) -> dict:
    seeds = jax.random.split(jax.random.key(seed), 10)
    att_query = draw_att_query(jax.random.fold_in(seeds[9], 71), 0)
    att_key = draw_att_key(jax.random.fold_in(seeds[9], 71), 0)
    att_value = gaussian(seeds[2], (SEQUENCE_TOKENS, HEAD_TOTAL, DH), 1.0, 6.0, ((0, 8), (1, 4)))
    norm_gain = jnp.clip(1.0 + 0.18 * jax.random.normal(seeds[3], (HEAD_TOTAL, DH), jnp.float32), 0.1, 1.9)
    dn_query = gaussian(seeds[4], (SEQUENCE_TOKENS, HEAD_TOTAL, DH), 1.0, 6.0, ((0, 8), (1, 4)))
    dn_key = draw_dn_key(jax.random.fold_in(seeds[9], 71), 0)
    write_rate = draw_write_rate(jax.random.fold_in(seeds[9], 71), 0)
    log_decay = draw_log_decay(jax.random.fold_in(seeds[9], 71), 0)
    out_grad = gaussian(seeds[8], (SEQUENCE_TOKENS, HEAD_TOTAL, DH), 1.0, 6.0, ((0, 8), (1, 4)))
    return dict(att_query=att_query, att_key=att_key, att_value=att_value, norm_gain=norm_gain, dn_query=dn_query, dn_key=dn_key, write_rate=write_rate, log_decay=log_decay, out_grad=out_grad)


MATMUL_ACCURACY = lax.Precision.HIGHEST
EPSILON = 1e-06

def unit_rows(matrix):
    return matrix * lax.rsqrt(lax.optimization_barrier(jnp.sum(matrix * matrix, axis=-1, keepdims=True)) + EPSILON)

def delta_block(memory_state, pieces):
    query_vectors, key_vectors, value_rows, rate_rows, decay_rows = pieces
    length = key_vectors.shape[1]
    lower = jnp.tril(jnp.ones((length, length), jnp.float32))
    strict = lower - jnp.eye(length, dtype=jnp.float32)
    running_state = jnp.cumsum(decay_rows, axis=1)
    ratio = jnp.exp((running_state[:, :, None] - running_state[:, None, :]) * lower) * lower
    state_increment = jnp.exp(running_state)
    intersection = jnp.einsum('htk,hsk->hts', key_vectors, key_vectors, precision=MATMUL_ACCURACY)
    system = jnp.eye(length, dtype=jnp.float32) + rate_rows[:, :, None] * ratio * strict * intersection
    retrieved_values = jnp.einsum('nex,nxp->nep', key_vectors, memory_state, precision=MATMUL_ACCURACY)
    target = rate_rows[:, :, None] * (value_rows - state_increment[:, :, None] * retrieved_values)
    newest_state = jax.scipy.linalg.solve_triangular(system, target, lower=True, unit_diagonal=True)
    local_scores = jnp.einsum('htk,hsk->hts', query_vectors, key_vectors, precision=MATMUL_ACCURACY) * ratio
    state_output = state_increment[:, :, None] * jnp.einsum('nex,nxp->nep', query_vectors, memory_state, precision=MATMUL_ACCURACY)
    state_output = state_output + jnp.einsum('hts,hsv->htv', local_scores, newest_state, precision=MATMUL_ACCURACY)
    retained_state = jnp.exp(running_state[:, -1:] - running_state)
    memory_state = jnp.exp(running_state[:, -1])[:, None, None] * memory_state + jnp.einsum('wpa,wpn->wan', key_vectors * retained_state[:, :, None], newest_state, precision=MATMUL_ACCURACY)
    return (memory_state, state_output)

def delta_sweep(memory_state, query_vectors, key_vectors, value_rows, rate_rows, decay_rows):
    head_count, length = (key_vectors.shape[0], key_vectors.shape[1])
    blocks = length // CH

    def cut_blocks(array):
        return jnp.moveaxis(array.reshape((head_count, blocks, CH) + array.shape[2:]), 1, 0)
    last_state, state_output = lax.scan(delta_block, memory_state, (cut_blocks(query_vectors), cut_blocks(key_vectors), cut_blocks(value_rows), cut_blocks(rate_rows), cut_blocks(decay_rows)))
    return (last_state, jnp.moveaxis(state_output, 0, 1).reshape(head_count, length, state_output.shape[-1]))

def window_softmax(rows_here, keys_here, values_here, alive_keys):
    block_rows = rows_here.shape[0]
    span_rows = keys_here.shape[0]
    reach_back = span_rows - block_rows
    scores = jnp.einsum('qhd,khd->hqk', rows_here, keys_here) * rows_here.shape[-1] ** (-0.5)
    query_pos = jnp.arange(block_rows, dtype=jnp.int32)[:, None]
    key_pos = jnp.arange(span_rows, dtype=jnp.int32)[None, :]
    allowed = (key_pos > query_pos) & (key_pos <= query_pos + reach_back) & alive_keys[None, :]
    scores = jnp.where(allowed[None], scores, -1e+30)
    shifted = jnp.exp(scores - lax.optimization_barrier(jnp.max(scores, axis=-1, keepdims=True)))
    weights_bf = (shifted / lax.optimization_barrier(jnp.sum(shifted, axis=-1, keepdims=True))).astype(jnp.bfloat16)
    return jnp.einsum('hqk,khd->qhd', weights_bf.astype(jnp.float32), values_here)

def all_attention(query_vectors, key_vectors, value_rows):
    block_rows = min(512, TOK_DEV)
    padding = jnp.zeros((WIN,) + key_vectors.shape[1:], jnp.float32)
    padded_keys = jnp.concatenate([padding, key_vectors], axis=0)
    padded_values = jnp.concatenate([padding, value_rows], axis=0)

    def one_block(block_index):
        first_row = block_index * block_rows
        rows_here = lax.dynamic_slice_in_dim(query_vectors, first_row, block_rows, 0)
        keys_here = lax.dynamic_slice_in_dim(padded_keys, first_row, block_rows + WIN, 0)
        values_here = lax.dynamic_slice_in_dim(padded_values, first_row, block_rows + WIN, 0)
        alive_keys = first_row + jnp.arange(block_rows + WIN, dtype=jnp.int32) >= WIN
        return window_softmax(rows_here, keys_here, values_here, alive_keys)
    outputs = lax.map(jax.checkpoint(one_block), jnp.arange(SEQUENCE_TOKENS // block_rows, dtype=jnp.int32))
    return outputs.reshape(SEQUENCE_TOKENS, HEAD_TOTAL, DH)

def reference(att_query, att_key, att_value, norm_gain, dn_query, dn_key, write_rate, log_decay, out_grad):

    def forward(query_in, key_in, value_in, gain_in, dq_in, dk_in, rate_in, decay_in):
        attended = all_attention(query_in.astype(jnp.float32), key_in.astype(jnp.float32), value_in.astype(jnp.float32))
        inverse = lax.rsqrt(lax.optimization_barrier(jnp.mean(attended * attended, axis=(1, 2))) + EPSILON)
        values = (attended * inverse[:, None, None] * gain_in[None]).astype(jnp.bfloat16)
        start_state = jnp.zeros((HEAD_TOTAL, DH, DH), jnp.float32)
        unit_query = unit_rows(jnp.swapaxes(dq_in, 0, 1).astype(jnp.float32))
        unit_key = unit_rows(jnp.swapaxes(dk_in, 0, 1).astype(jnp.float32))
        last_state, state_output = delta_sweep(start_state, unit_query, unit_key, jnp.swapaxes(values, 0, 1).astype(jnp.float32), rate_in.T, decay_in.T)
        return jnp.swapaxes(state_output, 0, 1)
    state_output, pullback = jax.vjp(forward, att_query, att_key, att_value, norm_gain, dn_query, dn_key, write_rate, log_decay)
    grads = pullback(out_grad.astype(jnp.float32))
    return (state_output.astype(jnp.bfloat16), grads[0], grads[1], grads[2], grads[3], grads[4], grads[5], grads[6], grads[7])
```

```python
import functools

import jax
import jax.numpy as jnp
from jax import lax
from jax.experimental import pallas as pl
from jax.experimental.pallas import tpu as pltpu
from jax.sharding import PartitionSpec as P

WIN = 1024
EPSILON = 1e-06
MESH = pl.DeviceIdType.MESH
F32 = jnp.float32
BF = jnp.bfloat16
NN = (((1,), (0,)), ((), ()))
NT = (((1,), (1,)), ((), ()))
TN = (((0,), (0,)), ((), ()))


def dot(a, b, dims=NN):
    return lax.dot_general(a.astype(BF), b.astype(BF), dims, preferred_element_type=F32)


def halves(a):
    high = a.astype(BF)
    return high, (a - high.astype(F32)).astype(BF)


def dot3(a, b, dims=NN):
    if a.dtype == BF and b.dtype == BF:
        return dot(a, b, dims)
    if a.dtype == BF:
        bh, bl = halves(b)
        return dot(a, bh, dims) + dot(a, bl, dims)
    if b.dtype == BF:
        ah, al = halves(a)
        return dot(ah, b, dims) + dot(al, b, dims)
    ah, al = halves(a)
    bh, bl = halves(b)
    return dot(ah, bh, dims) + (dot(ah, bl, dims) + dot(al, bh, dims))


def row_sum(a):
    return jnp.sum(a, axis=1, keepdims=True)


def col_sum(a):
    return jnp.sum(a, axis=0, keepdims=True)


def kernel(
    seq_n, head_n, reach, rounds, heads, width,
    q_ref, k_ref, v_ref, gain_ref, dq_ref, dk_ref, rate_ref, decay_ref, og_ref,
    out_ref, qg_ref, kg_ref, vg_ref, gg_ref, dqg_ref, dkg_ref, rg_ref, cg_ref,
    kv_in, fm_out, fm_in, fa_out, fa_in, bk_out, bk_in, hs_out, hs_in, gn_out, gn_in, gr_out, gr_in,
    t_s, ratio_s, p_s, kkr_s, score_s, weight_s,
    kv_ss, kv_rs, fm_ss, fm_rs, fa_ss, fa_rs, bk_ss, bk_rs, hs_ss, hs_rs, gn_ss, gn_rs, gr_ss, gr_rs,
):
    rows = q_ref.shape[0]
    me = lax.axis_index("seq")
    my_head = lax.axis_index("head")
    cols = [slice(h * width, (h + 1) * width) for h in range(heads)]

    def seq_copy(src, dst, send_sem, recv_sem, shift):
        target = lax.rem(me + (shift + seq_n), seq_n)
        return pltpu.make_async_remote_copy(
            src_ref=src, dst_ref=dst, send_sem=send_sem, recv_sem=recv_sem,
            device_id={"seq": target}, device_id_type=MESH,
        )

    def head_copy(step):
        target = lax.rem(my_head + step, head_n)
        return pltpu.make_async_remote_copy(
            src_ref=hs_out, dst_ref=hs_in.at[step - 1], send_sem=hs_ss.at[step - 1],
            recv_sem=hs_rs.at[step - 1], device_id={"head": target}, device_id_type=MESH,
        )

    def kv_copies(b):
        return [
            seq_copy(ref, kv_in.at[b - 1, i], kv_ss.at[b - 1, i], kv_rs.at[b - 1, i], b)
            for i, ref in enumerate((k_ref, v_ref))
        ]

    def grad_copies(b):
        return [
            seq_copy(gr_out.at[b - 1, i], gr_in.at[b - 1, i], gr_ss.at[b - 1, i], gr_rs.at[b - 1, i], -b)
            for i in range(2)
        ]

    def fm_copy(r):
        return seq_copy(fm_out.at[r], fm_in.at[r], fm_ss.at[r], fm_rs.at[r], 1 << r)

    def fa_copy(r):
        return seq_copy(fa_out.at[r], fa_in.at[r], fa_ss.at[r], fa_rs.at[r], 1 << r)

    def bk_copy(r):
        return seq_copy(bk_out.at[r], bk_in.at[r], bk_ss.at[r], bk_rs.at[r], -(1 << r))

    def gain_copy(step):
        return seq_copy(gn_out, gn_in.at[step - 1], gn_ss.at[step - 1], gn_rs.at[step - 1], step)

    def up_ok(d):
        return me + d < seq_n

    def down_ok(d):
        return me - d >= 0

    def start_if(condition, copies):
        @pl.when(condition)
        def _():
            for copy in copies:
                copy.start()

    def recv_if(condition, copies):
        @pl.when(condition)
        def _():
            for copy in copies:
                copy.wait_recv()

    def send_wait_if(condition, copies):
        @pl.when(condition)
        def _():
            for copy in copies:
                copy.wait_send()

    for b in range(1, reach + 1):
        @pl.when(jnp.logical_not(down_ok(b)))
        def _():
            kv_in[b - 1] = jnp.zeros(kv_in.shape[1:], BF)

        @pl.when(jnp.logical_not(up_ok(b)))
        def _():
            gr_in[b - 1] = jnp.zeros(gr_in.shape[1:], BF)
    for r in range(rounds):
        @pl.when(jnp.logical_not(down_ok(1 << r)))
        def _():
            fm_in[r] = jnp.zeros(fm_in.shape[1:], BF)
            fa_in[r] = jnp.zeros(fa_in.shape[1:], BF)

        @pl.when(jnp.logical_not(up_ok(1 << r)))
        def _():
            bk_in[r] = jnp.zeros(bk_in.shape[1:], BF)

    barrier = pltpu.get_barrier_semaphore()
    for step in range(1, seq_n):
        pl.semaphore_signal(barrier, inc=1, device_id={"seq": lax.rem(me + step, seq_n)}, device_id_type=MESH)
    for step in range(1, head_n):
        pl.semaphore_signal(barrier, inc=1, device_id={"head": lax.rem(my_head + step, head_n)}, device_id_type=MESH)
    pl.semaphore_wait(barrier, seq_n + head_n - 2)

    for b in range(1, reach + 1):
        start_if(up_ok(b), kv_copies(b))

    at_row = lax.broadcasted_iota(jnp.int32, (rows, rows), 0)
    at_col = lax.broadcasted_iota(jnp.int32, (rows, rows), 1)
    lower = at_row >= at_col
    strict = at_row > at_col
    diagonal = at_row == at_col
    eye = diagonal.astype(F32)

    def to_row(column):
        return col_sum(jnp.where(diagonal, column, 0.0))

    def to_col(line):
        return row_sum(jnp.where(diagonal, line, 0.0))

    state = []
    for h in range(heads):
        xq, xk, dout = dq_ref[:, cols[h]], dk_ref[:, cols[h]], og_ref[:, cols[h]]
        fq, fk = xq.astype(F32), xk.astype(F32)
        rq = lax.rsqrt(row_sum(fq * fq) + EPSILON)
        rk = lax.rsqrt(row_sum(fk * fk) + EPSILON)
        rk_row = to_row(rk)
        rate = rate_ref[:, h : h + 1]
        decay_row = to_row(decay_ref[:, h : h + 1])
        cum = row_sum(jnp.where(lower, decay_row, 0.0))
        cum_row = to_row(cum)
        ratio = jnp.where(lower, jnp.exp(jnp.where(lower, cum - cum_row, 0.0)), 0.0)
        gamma = jnp.exp(cum)
        last = cum[rows - 1 : rows, :]
        retain = jnp.exp(last - cum)
        whole = jnp.exp(last)
        kkr = dot(xk, xk, NT) * (rk * rk_row) * ratio
        p = dot(xq, xk, NT) * (rq * rk_row) * ratio
        ratio_s[h] = ratio
        kkr_s[h] = kkr
        p_s[h] = p
        system = jnp.where(strict, rate * kkr, 0.0)
        state.append(dict(
            rq=rq, rk=rk, rate=rate, gamma=gamma, retain=retain, whole=whole,
            q=fq * rq, k=fk * rk, system=system, dout=dout,
        ))
    inverse_of = []
    for h in range(heads):
        off = ((at_row >> 1) == (at_col >> 1))
        inverse_of.append(eye - jnp.where(off, state[h]["system"], 0.0))
    level = 1
    while (1 << level) < rows:
        off = ((at_row >> (level + 1)) == (at_col >> (level + 1))) & ((at_row >> level) != (at_col >> level))
        for h in range(heads):
            x = inverse_of[h]
            y = dot3(x, jnp.where(off, state[h]["system"], 0.0))
            inverse_of[h] = x - dot3(y, x)
        level += 1
    for h in range(heads):
        s = state[h]
        t = inverse_of[h]
        t_s[h] = t
        kr = s["k"] * s["retain"]
        w = dot3(t, s["rate"] * s["gamma"] * s["k"])
        y = s["gamma"] * s["q"] - dot3(p_s[h], w)
        small = lax.broadcasted_iota(jnp.int32, (width, width), 0) == lax.broadcasted_iota(jnp.int32, (width, width), 1)
        diag = jnp.where(small, s["whole"], 0.0)
        s["kr"], s["w"] = kr, w
        s["fm"] = diag - dot3(kr, w, TN)
        s["bm"] = diag - dot3(w, kr, TN)
        s["bb"] = dot3(y, s["dout"], TN)
        s["em"] = s["ea"] = s["eb"] = s["ebm"] = None

    def block(h, part=0, parts=1):
        return slice((part * heads + h) * width, (part * heads + h + 1) * width)

    def forward_send(r):
        for h in range(heads):
            fm_out[r, block(h)] = state[h]["fm"].astype(BF)
        start_if(up_ok(1 << r), [fm_copy(r)])

    def back_send(r):
        for h in range(heads):
            bk_out[r, block(h)] = state[h]["bm"].astype(BF)
            bk_out[r, block(h, 1)] = state[h]["bb"].astype(BF)
        start_if(down_ok(1 << r), [bk_copy(r)])

    def back_take(r):
        recv_if(up_ok(1 << r), [bk_copy(r)])
        for h in range(heads):
            s = state[h]
            m, b = bk_in[r, block(h)], bk_in[r, block(h, 1)]
            if r == 0:
                s["ebm"], s["eb"] = m.astype(F32), b.astype(F32)
            else:
                s["eb"] = s["eb"] + dot(s["ebm"], b)
                if r < rounds - 1:
                    s["ebm"] = dot(s["ebm"], m)
            if r < rounds - 1:
                s["bb"] = s["bb"] + dot(s["bm"], b)
                s["bm"] = dot(s["bm"], m)

    def forward_take(r):
        recv_if(down_ok(1 << r), [fm_copy(r)])
        for h in range(heads):
            s = state[h]
            m = fm_in[r, block(h)]
            s.setdefault("own", []).append(s["fm"])
            if r == 0:
                s["before"] = [None, m.astype(F32)]
            else:
                s["before"].append(dot(s["before"][-1], m) if r < rounds - 1 else None)
            if r < rounds - 1:
                s["fm"] = dot(s["fm"], m)

    scale = width ** (-0.5)

    def score_block(b):
        if b > 0:
            recv_if(down_ok(b), kv_copies(b))
        for h in range(heads):
            keys = k_ref[:, cols[h]] if b == 0 else kv_in[b - 1, 0, :, cols[h]]
            sc = dot(q_ref[:, cols[h]], keys, NT) * scale
            if b == 0:
                sc = jnp.where(lower, sc, -1e30)
            elif b == reach:
                sc = jnp.where(jnp.logical_and(at_col > at_row, down_ok(b)), sc, -1e30)
            else:
                sc = jnp.where(down_ok(b), sc, -1e30)
            score_s[h, b] = sc

    back_send(0)
    forward_send(0)
    score_block(0)
    for r in range(rounds):
        back_take(r)
        if r < rounds - 1:
            back_send(r + 1)
        forward_take(r)
        if r < rounds - 1:
            forward_send(r + 1)
    for h in range(heads):
        s = state[h]
        dn = dot3(p_s[h], s["dout"], TN) + dot3(s["kr"], s["eb"])
        s["r"] = dot3(t_s[h], dn, TN)
        s["vg"] = (s["rate"] * s["r"]).astype(BF).astype(F32)
    for b in range(1, reach + 1):
        score_block(b)
    square = 0.0
    inner = 0.0
    for h in range(heads):
        s = state[h]
        top = row_sum(jnp.zeros((rows, 128), F32)) - 1e30
        for b in range(reach + 1):
            top = jnp.maximum(top, jnp.max(score_s[h, b], axis=1, keepdims=True))
        total = 0.0
        for b in range(reach + 1):
            e = jnp.exp(score_s[h, b] - top)
            score_s[h, b] = e
            total = total + row_sum(e)
        attended = 0.0
        for b in range(reach + 1):
            w = score_s[h, b] / total
            score_s[h, b] = w
            wb = w.astype(BF)
            weight_s[h, b] = wb
            values = v_ref[:, cols[h]] if b == 0 else kv_in[b - 1, 1, :, cols[h]]
            attended = attended + dot(wb, values)
        s["att"] = attended
        s["weighted"] = s["vg"] * gain_ref[h : h + 1, :]
        square = square + row_sum(attended * attended)
        inner = inner + row_sum(s["weighted"] * attended)
    hs_out[0:8] = jnp.broadcast_to(to_row(square), (8, rows))
    hs_out[8:16] = jnp.broadcast_to(to_row(inner), (8, rows))
    for step in range(1, head_n):
        head_copy(step).start()
    sums = hs_out[...]
    for step in range(1, head_n):
        head_copy(step).wait_recv()
        sums = sums + hs_in[step - 1]
    features = heads * head_n * width
    inverse = lax.rsqrt(to_col(sums[0:1]) / features + EPSILON)
    slope = inverse * inverse * inverse * to_col(sums[8:9]) / features
    gains = []
    for h in range(heads):
        s = state[h]
        scaled = s["att"] * inverse
        gains.append(col_sum(s["vg"] * scaled))
        s["val"] = (scaled * gain_ref[h : h + 1, :]).astype(BF)
        s["datt"] = (inverse * s["weighted"] - s["att"] * slope).astype(BF)
        s["u0"] = dot3(t_s[h], s["rate"] * s["val"].astype(F32))
        s["fa"] = dot3(s["kr"], s["u0"], TN)

    def add_send(r):
        for h in range(heads):
            fa_out[r, block(h)] = state[h]["fa"].astype(BF)
        start_if(up_ok(1 << r), [fa_copy(r)])

    def add_take(r):
        recv_if(down_ok(1 << r), [fa_copy(r)])
        for h in range(heads):
            s = state[h]
            a = fa_in[r, block(h)]
            s["ea"] = a.astype(F32) if r == 0 else s["ea"] + dot(s["before"][r], a)
            if r < rounds - 1:
                s["fa"] = s["fa"] + dot(s["own"][r], a)

    add_send(0)
    gn_out[...] = jnp.concatenate(gains + [jnp.zeros((8 - heads, width), F32)], axis=0)
    for step in range(1, seq_n):
        gain_copy(step).start()

    for h in range(heads):
        s = state[h]
        mean = 0.0
        for b in range(reach + 1):
            values = v_ref[:, cols[h]] if b == 0 else kv_in[b - 1, 1, :, cols[h]]
            dw = dot(s["datt"], values, NT).astype(BF).astype(F32)
            mean = mean + row_sum(dw * score_s[h, b])
        s["mean"] = mean
        s["dqa"] = 0.0
    own_grad = []
    for b in list(range(reach, 0, -1)) + [0]:
        for h in range(heads):
            s = state[h]
            keys = k_ref[:, cols[h]] if b == 0 else kv_in[b - 1, 0, :, cols[h]]
            values = v_ref[:, cols[h]] if b == 0 else kv_in[b - 1, 1, :, cols[h]]
            dw = dot(s["datt"], values, NT).astype(BF).astype(F32)
            ds = (score_s[h, b] * (dw - s["mean"]) * scale).astype(BF)
            s["dqa"] = s["dqa"] + dot(ds, keys)
            dkey = dot(ds, q_ref[:, cols[h]], TN)
            dval = dot(weight_s[h, b], s["datt"], TN)
            if b > 0:
                gr_out[b - 1, 0, :, cols[h]] = dkey.astype(BF)
                gr_out[b - 1, 1, :, cols[h]] = dval.astype(BF)
            else:
                own_grad.append((dkey, dval))
        if b > 0:
            start_if(down_ok(b), grad_copies(b))
        if reach - b < rounds and b > 0:
            r = reach - b
            add_take(r)
            if r < rounds - 1:
                add_send(r + 1)
    for r in range(reach, rounds):
        add_take(r)
        if r < rounds - 1:
            add_send(r + 1)
    for h in range(heads):
        qg_ref[:, cols[h]] = state[h]["dqa"].astype(BF)

    for h in range(heads):
        s = state[h]
        start, later = s["ea"], s["eb"]
        q, k, rate, gamma, retain = s["q"], s["k"], s["rate"], s["gamma"], s["retain"]
        r, dout = s["r"], s["dout"]
        fout = dout.astype(F32)
        ks = dot(k, start)
        qs = dot(q, start)
        new = s["u0"] - dot3(s["w"], start)
        p = p_s[h]
        out_ref[:, cols[h]] = (gamma * qs + dot(p, new)).astype(BF)
        dp = dot(dout, new, NT)
        da = jnp.where(strict, -dot(r, new, NT), 0.0)
        ratio, kkr = ratio_s[h], kkr_s[h]
        dqk = (dp * ratio)
        dkk = da * (rate * ratio)
        ak = da * kkr
        e = dp * p + ak * rate
        vals = s["val"].astype(F32)
        rate_grad = row_sum(ak) + row_sum(r * (vals - gamma * ks))
        down = -rate * r
        dgamma = row_sum(down * ks + fout * qs)
        dks = gamma * down
        dq = dot(gamma * fout, start, NT) + dot(dqk, k)
        dkr = dot(new, later, NT)
        dk = (
            dot(dks, start, NT) + dot(dqk, q, TN) + dot(dkk, k) + dot(dkk, k, TN) + retain * dkr
        )
        dret = row_sum(dkr * k) * retain
        dlast = col_sum(dret) + s["whole"] * col_sum(row_sum(later * start))
        dcum = to_row(row_sum(e) + dgamma * gamma - dret) - col_sum(e)
        cg_ref[:, h : h + 1] = row_sum(jnp.where(at_col >= at_row, dcum, 0.0)) + dlast
        rg_ref[:, h : h + 1] = rate_grad
        dqg_ref[:, cols[h]] = (s["rq"] * (dq - q * row_sum(q * dq))).astype(BF)
        dkg_ref[:, cols[h]] = (s["rk"] * (dk - k * row_sum(k * dk))).astype(BF)

    gain = gn_out[...]
    for step in range(1, seq_n):
        gain_copy(step).wait_recv()
        gain = gain + gn_in[step - 1]
    gg_ref[...] = gain[0:heads]
    for b in range(reach, 0, -1):
        recv_if(up_ok(b), grad_copies(b))
    for h in range(heads):
        dkey, dval = own_grad[h]
        for b in range(1, reach + 1):
            dkey = dkey + gr_in[b - 1, 0, :, cols[h]].astype(F32)
            dval = dval + gr_in[b - 1, 1, :, cols[h]].astype(F32)
        kg_ref[:, cols[h]] = dkey.astype(BF)
        vg_ref[:, cols[h]] = dval.astype(BF)

    for b in range(1, reach + 1):
        send_wait_if(up_ok(b), kv_copies(b))
        send_wait_if(down_ok(b), grad_copies(b))
    for r in range(rounds):
        send_wait_if(up_ok(1 << r), [fm_copy(r), fa_copy(r)])
        send_wait_if(down_ok(1 << r), [bk_copy(r)])
    for step in range(1, head_n):
        head_copy(step).wait_send()
    for step in range(1, seq_n):
        gain_copy(step).wait_send()


def body(att_query, att_key, att_value, norm_gain, dn_query, dn_key, write_rate, log_decay, out_grad):
    rows, heads, width = att_query.shape
    seq_n, head_n = lax.axis_size("seq"), lax.axis_size("head")
    reach = max(1, WIN // rows)
    rounds = max(1, (seq_n - 1).bit_length())
    wide = heads * width

    def flat(a):
        return a.reshape(rows, wide)

    big = jax.ShapeDtypeStruct((rows, wide), BF)
    thin = jax.ShapeDtypeStruct((rows, heads), F32)
    outs = [big, big, big, big, jax.ShapeDtypeStruct((heads, width), F32), big, big, thin, thin]
    dma = pltpu.SemaphoreType.DMA
    scratch = [
        pltpu.VMEM((reach, 2, rows, wide), BF),
        pltpu.VMEM((rounds, wide, width), BF),
        pltpu.VMEM((rounds, wide, width), BF),
        pltpu.VMEM((rounds, wide, width), BF),
        pltpu.VMEM((rounds, wide, width), BF),
        pltpu.VMEM((rounds, 2 * wide, width), BF),
        pltpu.VMEM((rounds, 2 * wide, width), BF),
        pltpu.VMEM((16, rows), F32),
        pltpu.VMEM((max(1, head_n - 1), 16, rows), F32),
        pltpu.VMEM((8, width), F32),
        pltpu.VMEM((max(1, seq_n - 1), 8, width), F32),
        pltpu.VMEM((reach, 2, rows, wide), BF),
        pltpu.VMEM((reach, 2, rows, wide), BF),
        pltpu.VMEM((heads, rows, rows), F32),
        pltpu.VMEM((heads, rows, rows), F32),
        pltpu.VMEM((heads, rows, rows), F32),
        pltpu.VMEM((heads, rows, rows), F32),
        pltpu.VMEM((heads, reach + 1, rows, rows), F32),
        pltpu.VMEM((heads, reach + 1, rows, rows), BF),
        dma((reach, 2)), dma((reach, 2)),
        dma((rounds,)), dma((rounds,)),
        dma((rounds,)), dma((rounds,)),
        dma((rounds,)), dma((rounds,)),
        dma((max(1, head_n - 1),)), dma((max(1, head_n - 1),)),
        dma((max(1, seq_n - 1),)), dma((max(1, seq_n - 1),)),
        dma((reach, 2)), dma((reach, 2)),
    ]
    vmem = pl.BlockSpec(memory_space=pltpu.VMEM)
    results = pl.pallas_call(
        functools.partial(kernel, seq_n, head_n, reach, rounds, heads, width),
        out_shape=outs,
        in_specs=[vmem] * 9,
        out_specs=[vmem] * 9,
        scratch_shapes=scratch,
        compiler_params=pltpu.CompilerParams(
            collective_id=0, has_side_effects=True, vmem_limit_bytes=48 * 1024 * 1024
        ),
    )(
        flat(att_query), flat(att_key), flat(att_value), norm_gain, flat(dn_query), flat(dn_key),
        write_rate, log_decay, flat(out_grad),
    )

    def tall(a):
        return a.reshape(rows, heads, width)

    o, qg, kg, vg, gg, dqg, dkg, rg, cg = results
    return (tall(o), tall(qg), tall(kg), tall(vg), gg, tall(dqg), tall(dkg), rg, cg)


def solution(mesh):
    cube = P("seq", "head", None)
    pair = P("seq", "head")
    return jax.shard_map(
        body,
        mesh=mesh,
        in_specs=(cube, cube, cube, P("head", None), cube, cube, pair, pair, cube),
        out_specs=(cube, cube, cube, cube, P("head", None), cube, cube, pair, pair),
        check_vma=False,
    )
```

```python
import functools

import jax
import jax.numpy as jnp
from jax import lax
from jax.experimental import pallas as pl
from jax.experimental.pallas import tpu as pltpu
from jax.sharding import PartitionSpec as P

WIN = 1024
EPSILON = 1e-06
MESH = pl.DeviceIdType.MESH
F32 = jnp.float32
BF = jnp.bfloat16
NN = (((1,), (0,)), ((), ()))
NT = (((1,), (1,)), ((), ()))
TN = (((0,), (0,)), ((), ()))


def dot(a, b, dims=NN):
    return lax.dot_general(a.astype(BF), b.astype(BF), dims, preferred_element_type=F32)


def halves(a):
    high = a.astype(BF)
    return high, (a - high.astype(F32)).astype(BF)


def dot3(a, b, dims=NN):
    if a.dtype == BF and b.dtype == BF:
        return dot(a, b, dims)
    if a.dtype == BF:
        bh, bl = halves(b)
        return dot(a, bh, dims) + dot(a, bl, dims)
    if b.dtype == BF:
        ah, al = halves(a)
        return dot(ah, b, dims) + dot(al, b, dims)
    ah, al = halves(a)
    bh, bl = halves(b)
    return dot(ah, bh, dims) + (dot(ah, bl, dims) + dot(al, bh, dims))


def row_sum(a):
    return jnp.sum(a, axis=1, keepdims=True)


def col_sum(a):
    return jnp.sum(a, axis=0, keepdims=True)


def kernel(
    seq_n, head_n, reach, rounds, heads, width,
    q_ref, k_ref, v_ref, gain_ref, dq_ref, dk_ref, rate_ref, decay_ref, og_ref,
    out_ref, qg_ref, kg_ref, vg_ref, gg_ref, dqg_ref, dkg_ref, rg_ref, cg_ref,
    kv_in, fm_out, fm_in, fa_out, fa_in, bk_out, bk_in, hs_out, hs_in, gn_out, gn_in, gr_out, gr_in, gx_in,
    t_s, ratio_s, p_s, kkr_s, score_s, weight_s,
    kv_ss, kv_rs, fm_ss, fm_rs, fa_ss, fa_rs, bk_ss, bk_rs, hs_ss, hs_rs, gn_ss, gn_rs, gr_ss, gr_rs,
):
    rows = q_ref.shape[0]
    me = lax.axis_index("seq")
    my_head = lax.axis_index("head")
    cols = [slice(h * width, (h + 1) * width) for h in range(heads)]

    def seq_copy(src, dst, send_sem, recv_sem, shift):
        target = lax.rem(me + (shift + seq_n), seq_n)
        return pltpu.make_async_remote_copy(
            src_ref=src, dst_ref=dst, send_sem=send_sem, recv_sem=recv_sem,
            device_id={"seq": target}, device_id_type=MESH,
        )

    def head_copy(step):
        target = lax.rem(my_head + step, head_n)
        return pltpu.make_async_remote_copy(
            src_ref=hs_out, dst_ref=hs_in.at[step - 1], send_sem=hs_ss.at[step - 1],
            recv_sem=hs_rs.at[step - 1], device_id={"head": target}, device_id_type=MESH,
        )

    def kv_copies(b):
        return [
            seq_copy(ref, kv_in.at[b - 1, i], kv_ss.at[b - 1, i], kv_rs.at[b - 1, i], b)
            for i, ref in enumerate((k_ref, v_ref))
        ]

    odd = lax.rem(me, 2) == 1
    even = jnp.logical_not(odd)
    partner = me + 1 - 2 * lax.rem(me, 2)

    def partner_copy(src, dst, send_sem, recv_sem):
        return pltpu.make_async_remote_copy(
            src_ref=src, dst_ref=dst, send_sem=send_sem, recv_sem=recv_sem,
            device_id={"seq": partner}, device_id_type=MESH,
        )

    def hand_copies(b, slot):
        source = [k_ref, v_ref] if slot == 0 else [kv_in.at[slot - 1, i] for i in range(2)]
        return [
            partner_copy(source[i], kv_in.at[b - 1, i], kv_ss.at[b - 1, i], kv_rs.at[b - 1, i])
            for i in range(2)
        ]

    def cross_copies(b):
        return [
            partner_copy(gr_out.at[b - 1, i], gx_in.at[b - 1, i], gr_ss.at[b - 1, i], gr_rs.at[b - 1, i])
            for i in range(2)
        ]

    def grad_copies(b):
        return [
            seq_copy(gr_out.at[b - 1, i], gr_in.at[b - 1, i], gr_ss.at[b - 1, i], gr_rs.at[b - 1, i], -b)
            for i in range(2)
        ]

    def fm_copy(r):
        return seq_copy(fm_out.at[r], fm_in.at[r], fm_ss.at[r], fm_rs.at[r], 1 << r)

    def fa_copy(r):
        return seq_copy(fa_out.at[r], fa_in.at[r], fa_ss.at[r], fa_rs.at[r], 1 << r)

    def bk_copy(r):
        return seq_copy(bk_out.at[r], bk_in.at[r], bk_ss.at[r], bk_rs.at[r], -(1 << r))

    def gain_copy(step):
        return seq_copy(gn_out, gn_in.at[step - 1], gn_ss.at[step - 1], gn_rs.at[step - 1], step)

    def up_ok(d):
        return me + d < seq_n

    def down_ok(d):
        return me - d >= 0

    def start_if(condition, copies):
        @pl.when(condition)
        def _():
            for copy in copies:
                copy.start()

    def recv_if(condition, copies):
        @pl.when(condition)
        def _():
            for copy in copies:
                copy.wait_recv()

    def send_wait_if(condition, copies):
        @pl.when(condition)
        def _():
            for copy in copies:
                copy.wait_send()

    for b in range(1, reach + 1):
        @pl.when(jnp.logical_not(down_ok(b)))
        def _():
            kv_in[b - 1] = jnp.zeros(kv_in.shape[1:], BF)

        @pl.when(partner - b < 0)
        def _():
            gx_in[b - 1] = jnp.zeros(gx_in.shape[1:], BF)

        @pl.when(jnp.logical_not(up_ok(b)))
        def _():
            gr_in[b - 1] = jnp.zeros(gr_in.shape[1:], BF)
    for r in range(rounds):
        @pl.when(jnp.logical_not(down_ok(1 << r)))
        def _():
            fm_in[r] = jnp.zeros(fm_in.shape[1:], BF)
            fa_in[r] = jnp.zeros(fa_in.shape[1:], BF)

        @pl.when(jnp.logical_not(up_ok(1 << r)))
        def _():
            bk_in[r] = jnp.zeros(bk_in.shape[1:], BF)

    barrier = pltpu.get_barrier_semaphore()
    for step in range(1, seq_n):
        pl.semaphore_signal(barrier, inc=1, device_id={"seq": lax.rem(me + step, seq_n)}, device_id_type=MESH)
    for step in range(1, head_n):
        pl.semaphore_signal(barrier, inc=1, device_id={"head": lax.rem(my_head + step, head_n)}, device_id_type=MESH)
    pl.semaphore_wait(barrier, seq_n + head_n - 2)

    for b in range(2, reach + 1, 2):
        start_if(up_ok(b), kv_copies(b))
    start_if(even, hand_copies(1, 0))

    def hand_on(slot):
        recv_if(down_ok(slot), kv_copies(slot))
        if slot + 1 < reach:
            start_if(jnp.logical_and(even, partner - (slot + 1) >= 0), hand_copies(slot + 1, slot))
        start_if(jnp.logical_and(odd, partner - (slot - 1) >= 0), hand_copies(slot - 1, slot))

    at_row = lax.broadcasted_iota(jnp.int32, (rows, rows), 0)
    at_col = lax.broadcasted_iota(jnp.int32, (rows, rows), 1)
    lower = at_row >= at_col
    strict = at_row > at_col
    diagonal = at_row == at_col
    eye = diagonal.astype(F32)

    def to_row(column):
        return col_sum(jnp.where(diagonal, column, 0.0))

    def to_col(line):
        return row_sum(jnp.where(diagonal, line, 0.0))

    state = []
    for h in range(heads):
        xq, xk, dout = dq_ref[:, cols[h]], dk_ref[:, cols[h]], og_ref[:, cols[h]]
        fq, fk = xq.astype(F32), xk.astype(F32)
        rq = lax.rsqrt(row_sum(fq * fq) + EPSILON)
        rk = lax.rsqrt(row_sum(fk * fk) + EPSILON)
        rk_row = to_row(rk)
        rate = rate_ref[:, h : h + 1]
        decay_row = to_row(decay_ref[:, h : h + 1])
        cum = row_sum(jnp.where(lower, decay_row, 0.0))
        cum_row = to_row(cum)
        ratio = jnp.where(lower, jnp.exp(jnp.where(lower, cum - cum_row, 0.0)), 0.0)
        gamma = jnp.exp(cum)
        last = cum[rows - 1 : rows, :]
        retain = jnp.exp(last - cum)
        whole = jnp.exp(last)
        kkr = dot(xk, xk, NT) * (rk * rk_row) * ratio
        p = dot(xq, xk, NT) * (rq * rk_row) * ratio
        ratio_s[h] = ratio
        kkr_s[h] = kkr
        p_s[h] = p
        system = jnp.where(strict, rate * kkr, 0.0)
        state.append(dict(
            rq=rq, rk=rk, rate=rate, gamma=gamma, retain=retain, whole=whole,
            q=fq * rq, k=fk * rk, system=system, dout=dout,
        ))
    inverse_of = []
    for h in range(heads):
        off = ((at_row >> 1) == (at_col >> 1))
        inverse_of.append(eye - jnp.where(off, state[h]["system"], 0.0))
    level = 1
    while (1 << level) < rows:
        off = ((at_row >> (level + 1)) == (at_col >> (level + 1))) & ((at_row >> level) != (at_col >> level))
        for h in range(heads):
            x = inverse_of[h]
            y = dot3(x, jnp.where(off, state[h]["system"], 0.0))
            inverse_of[h] = x - dot3(y, x)
        level += 1
        if level == 5:
            hand_on(2)
    for slot in range(4, reach + 1, 2):
        hand_on(slot)
    for h in range(heads):
        s = state[h]
        t = inverse_of[h]
        t_s[h] = t
        kr = s["k"] * s["retain"]
        w = dot3(t, s["rate"] * s["gamma"] * s["k"])
        y = s["gamma"] * s["q"] - dot3(p_s[h], w)
        small = lax.broadcasted_iota(jnp.int32, (width, width), 0) == lax.broadcasted_iota(jnp.int32, (width, width), 1)
        diag = jnp.where(small, s["whole"], 0.0)
        s["kr"], s["w"] = kr, w
        s["fm"] = diag - dot3(kr, w, TN)
        s["bm"] = diag - dot3(w, kr, TN)
        s["bb"] = dot3(y, s["dout"], TN)
        s["em"] = s["ea"] = s["eb"] = s["ebm"] = None

    def block(h, part=0, parts=1):
        return slice((part * heads + h) * width, (part * heads + h + 1) * width)

    def forward_send(r):
        for h in range(heads):
            fm_out[r, block(h)] = state[h]["fm"].astype(BF)
        start_if(up_ok(1 << r), [fm_copy(r)])

    def back_send(r):
        for h in range(heads):
            bk_out[r, block(h)] = state[h]["bm"].astype(BF)
            bk_out[r, block(h, 1)] = state[h]["bb"].astype(BF)
        start_if(down_ok(1 << r), [bk_copy(r)])

    def back_take(r):
        recv_if(up_ok(1 << r), [bk_copy(r)])
        for h in range(heads):
            s = state[h]
            m, b = bk_in[r, block(h)], bk_in[r, block(h, 1)]
            if r == 0:
                s["ebm"], s["eb"] = m.astype(F32), b.astype(F32)
            else:
                s["eb"] = s["eb"] + dot(s["ebm"], b)
                if r < rounds - 1:
                    s["ebm"] = dot(s["ebm"], m)
            if r < rounds - 1:
                s["bb"] = s["bb"] + dot(s["bm"], b)
                s["bm"] = dot(s["bm"], m)

    def forward_take(r):
        recv_if(down_ok(1 << r), [fm_copy(r)])
        for h in range(heads):
            s = state[h]
            m = fm_in[r, block(h)]
            s.setdefault("own", []).append(s["fm"])
            if r == 0:
                s["before"] = [None, m.astype(F32)]
            else:
                s["before"].append(dot(s["before"][-1], m) if r < rounds - 1 else None)
            if r < rounds - 1:
                s["fm"] = dot(s["fm"], m)

    scale = width ** (-0.5)

    def score_block(b):
        if b % 2 == 1:
            recv_if(down_ok(b), hand_copies(b, 0))
        for h in range(heads):
            keys = k_ref[:, cols[h]] if b == 0 else kv_in[b - 1, 0, :, cols[h]]
            sc = dot(q_ref[:, cols[h]], keys, NT) * scale
            if b == 0:
                sc = jnp.where(lower, sc, -1e30)
            elif b == reach:
                sc = jnp.where(jnp.logical_and(at_col > at_row, down_ok(b)), sc, -1e30)
            else:
                sc = jnp.where(down_ok(b), sc, -1e30)
            score_s[h, b] = sc

    back_send(0)
    forward_send(0)
    score_block(0)
    for r in range(rounds):
        back_take(r)
        if r < rounds - 1:
            back_send(r + 1)
        forward_take(r)
        if r < rounds - 1:
            forward_send(r + 1)
    for h in range(heads):
        s = state[h]
        dn = dot3(p_s[h], s["dout"], TN) + dot3(s["kr"], s["eb"])
        s["r"] = dot3(t_s[h], dn, TN)
        s["vg"] = (s["rate"] * s["r"]).astype(BF).astype(F32)
    for b in list(range(2, reach + 1, 2)) + list(range(1, reach + 1, 2)):
        score_block(b)
    square = 0.0
    inner = 0.0
    for h in range(heads):
        s = state[h]
        top = row_sum(jnp.zeros((rows, 128), F32)) - 1e30
        for b in range(reach + 1):
            top = jnp.maximum(top, jnp.max(score_s[h, b], axis=1, keepdims=True))
        total = 0.0
        for b in range(reach + 1):
            e = jnp.exp(score_s[h, b] - top)
            score_s[h, b] = e
            total = total + row_sum(e)
        attended = 0.0
        for b in range(reach + 1):
            w = score_s[h, b] / total
            score_s[h, b] = w
            wb = w.astype(BF)
            weight_s[h, b] = wb
            values = v_ref[:, cols[h]] if b == 0 else kv_in[b - 1, 1, :, cols[h]]
            attended = attended + dot(wb, values)
        s["att"] = attended
        s["weighted"] = s["vg"] * gain_ref[h : h + 1, :]
        square = square + row_sum(attended * attended)
        inner = inner + row_sum(s["weighted"] * attended)
    hs_out[0:8] = jnp.broadcast_to(to_row(square), (8, rows))
    hs_out[8:16] = jnp.broadcast_to(to_row(inner), (8, rows))
    for step in range(1, head_n):
        head_copy(step).start()
    sums = hs_out[...]
    for step in range(1, head_n):
        head_copy(step).wait_recv()
        sums = sums + hs_in[step - 1]
    features = heads * head_n * width
    inverse = lax.rsqrt(to_col(sums[0:1]) / features + EPSILON)
    slope = inverse * inverse * inverse * to_col(sums[8:9]) / features
    gains = []
    for h in range(heads):
        s = state[h]
        scaled = s["att"] * inverse
        gains.append(col_sum(s["vg"] * scaled))
        s["val"] = (scaled * gain_ref[h : h + 1, :]).astype(BF)
        s["datt"] = (inverse * s["weighted"] - s["att"] * slope).astype(BF)
        s["u0"] = dot3(t_s[h], s["rate"] * s["val"].astype(F32))
        s["fa"] = dot3(s["kr"], s["u0"], TN)

    def add_send(r):
        for h in range(heads):
            fa_out[r, block(h)] = state[h]["fa"].astype(BF)
        start_if(up_ok(1 << r), [fa_copy(r)])

    def add_take(r):
        recv_if(down_ok(1 << r), [fa_copy(r)])
        for h in range(heads):
            s = state[h]
            a = fa_in[r, block(h)]
            s["ea"] = a.astype(F32) if r == 0 else s["ea"] + dot(s["before"][r], a)
            if r < rounds - 1:
                s["fa"] = s["fa"] + dot(s["own"][r], a)

    add_send(0)
    gn_out[...] = jnp.concatenate(gains + [jnp.zeros((8 - heads, width), F32)], axis=0)
    for step in range(1, seq_n):
        gain_copy(step).start()

    for h in range(heads):
        s = state[h]
        mean = 0.0
        for b in range(reach + 1):
            values = v_ref[:, cols[h]] if b == 0 else kv_in[b - 1, 1, :, cols[h]]
            dw = dot(s["datt"], values, NT).astype(BF).astype(F32)
            mean = mean + row_sum(dw * score_s[h, b])
        s["mean"] = mean
        s["dqa"] = 0.0
    own_grad = []
    turn = 0
    for b in list(range(reach - 1, 0, -2)) + list(range(reach, 0, -2)) + [0]:
        for h in range(heads):
            s = state[h]
            keys = k_ref[:, cols[h]] if b == 0 else kv_in[b - 1, 0, :, cols[h]]
            values = v_ref[:, cols[h]] if b == 0 else kv_in[b - 1, 1, :, cols[h]]
            dw = dot(s["datt"], values, NT).astype(BF).astype(F32)
            ds = (score_s[h, b] * (dw - s["mean"]) * scale).astype(BF)
            s["dqa"] = s["dqa"] + dot(ds, keys)
            dkey = dot(ds, q_ref[:, cols[h]], TN)
            dval = dot(weight_s[h, b], s["datt"], TN)
            if b > 0:
                gr_out[b - 1, 0, :, cols[h]] = dkey.astype(BF)
                gr_out[b - 1, 1, :, cols[h]] = dval.astype(BF)
            else:
                own_grad.append((dkey, dval))
        if b % 2 == 1:
            start_if(down_ok(b), cross_copies(b))
        if turn < rounds:
            add_take(turn)
            if turn < rounds - 1:
                add_send(turn + 1)
        turn += 1
    for r in range(turn, rounds):
        add_take(r)
        if r < rounds - 1:
            add_send(r + 1)
    for h in range(heads):
        qg_ref[:, cols[h]] = state[h]["dqa"].astype(BF)

    def cross_add(b):
        recv_if(partner - b >= 0, cross_copies(b))
        if b > 1:
            @pl.when(jnp.logical_and(even, down_ok(b - 1)))
            def _():
                total = gr_out[b - 2].astype(F32) + gx_in[b - 1].astype(F32)
                gr_out[b - 2] = total.astype(BF)

        @pl.when(jnp.logical_and(odd, down_ok(b + 1)))
        def _():
            total = gr_out[b].astype(F32) + gx_in[b - 1].astype(F32)
            gr_out[b] = total.astype(BF)

    def finish(h):
        s = state[h]
        start, later = s["ea"], s["eb"]
        q, k, rate, gamma, retain = s["q"], s["k"], s["rate"], s["gamma"], s["retain"]
        r, dout = s["r"], s["dout"]
        fout = dout.astype(F32)
        ks = dot(k, start)
        qs = dot(q, start)
        new = s["u0"] - dot3(s["w"], start)
        p = p_s[h]
        out_ref[:, cols[h]] = (gamma * qs + dot(p, new)).astype(BF)
        dp = dot(dout, new, NT)
        da = jnp.where(strict, -dot(r, new, NT), 0.0)
        ratio, kkr = ratio_s[h], kkr_s[h]
        dqk = (dp * ratio)
        dkk = da * (rate * ratio)
        ak = da * kkr
        e = dp * p + ak * rate
        vals = s["val"].astype(F32)
        rate_grad = row_sum(ak) + row_sum(r * (vals - gamma * ks))
        down = -rate * r
        dgamma = row_sum(down * ks + fout * qs)
        dks = gamma * down
        dq = dot(gamma * fout, start, NT) + dot(dqk, k)
        dkr = dot(new, later, NT)
        dk = (
            dot(dks, start, NT) + dot(dqk, q, TN) + dot(dkk, k) + dot(dkk, k, TN) + retain * dkr
        )
        dret = row_sum(dkr * k) * retain
        dlast = col_sum(dret) + s["whole"] * col_sum(row_sum(later * start))
        dcum = to_row(row_sum(e) + dgamma * gamma - dret) - col_sum(e)
        cg_ref[:, h : h + 1] = row_sum(jnp.where(at_col >= at_row, dcum, 0.0)) + dlast
        rg_ref[:, h : h + 1] = rate_grad
        dqg_ref[:, cols[h]] = (s["rq"] * (dq - q * row_sum(q * dq))).astype(BF)
        dkg_ref[:, cols[h]] = (s["rk"] * (dk - k * row_sum(k * dk))).astype(BF)

    for b in range(reach - 1, 0, -2):
        cross_add(b)
        start_if(down_ok(b + 1), grad_copies(b + 1))
    for h in range(heads):
        finish(h)

    gain = gn_out[...]
    for step in range(1, seq_n):
        gain_copy(step).wait_recv()
        gain = gain + gn_in[step - 1]
    gg_ref[...] = gain[0:heads]
    for b in range(reach, 0, -2):
        recv_if(up_ok(b), grad_copies(b))
    for h in range(heads):
        dkey, dval = own_grad[h]
        dkey = dkey + jnp.where(even, gx_in[0, 0, :, cols[h]].astype(F32), 0.0)
        dval = dval + jnp.where(even, gx_in[0, 1, :, cols[h]].astype(F32), 0.0)
        for b in range(2, reach + 1, 2):
            dkey = dkey + gr_in[b - 1, 0, :, cols[h]].astype(F32)
            dval = dval + gr_in[b - 1, 1, :, cols[h]].astype(F32)
        kg_ref[:, cols[h]] = dkey.astype(BF)
        vg_ref[:, cols[h]] = dval.astype(BF)

    for b in range(2, reach + 1, 2):
        send_wait_if(up_ok(b), kv_copies(b))
        send_wait_if(down_ok(b), grad_copies(b))
    for b in range(1, reach + 1, 2):
        send_wait_if(partner - b >= 0, hand_copies(b, 0))
        send_wait_if(down_ok(b), cross_copies(b))
    for r in range(rounds):
        send_wait_if(up_ok(1 << r), [fm_copy(r), fa_copy(r)])
        send_wait_if(down_ok(1 << r), [bk_copy(r)])
    for step in range(1, head_n):
        head_copy(step).wait_send()
    for step in range(1, seq_n):
        gain_copy(step).wait_send()


def body(att_query, att_key, att_value, norm_gain, dn_query, dn_key, write_rate, log_decay, out_grad):
    rows, heads, width = att_query.shape
    seq_n, head_n = lax.axis_size("seq"), lax.axis_size("head")
    reach = max(1, WIN // rows)
    rounds = max(1, (seq_n - 1).bit_length())
    wide = heads * width

    def flat(a):
        return a.reshape(rows, wide)

    big = jax.ShapeDtypeStruct((rows, wide), BF)
    thin = jax.ShapeDtypeStruct((rows, heads), F32)
    outs = [big, big, big, big, jax.ShapeDtypeStruct((heads, width), F32), big, big, thin, thin]
    dma = pltpu.SemaphoreType.DMA
    scratch = [
        pltpu.VMEM((reach, 2, rows, wide), BF),
        pltpu.VMEM((rounds, wide, width), BF),
        pltpu.VMEM((rounds, wide, width), BF),
        pltpu.VMEM((rounds, wide, width), BF),
        pltpu.VMEM((rounds, wide, width), BF),
        pltpu.VMEM((rounds, 2 * wide, width), BF),
        pltpu.VMEM((rounds, 2 * wide, width), BF),
        pltpu.VMEM((16, rows), F32),
        pltpu.VMEM((max(1, head_n - 1), 16, rows), F32),
        pltpu.VMEM((8, width), F32),
        pltpu.VMEM((max(1, seq_n - 1), 8, width), F32),
        pltpu.VMEM((reach, 2, rows, wide), BF),
        pltpu.VMEM((reach, 2, rows, wide), BF),
        pltpu.VMEM((reach, 2, rows, wide), BF),
        pltpu.VMEM((heads, rows, rows), F32),
        pltpu.VMEM((heads, rows, rows), F32),
        pltpu.VMEM((heads, rows, rows), F32),
        pltpu.VMEM((heads, rows, rows), F32),
        pltpu.VMEM((heads, reach + 1, rows, rows), F32),
        pltpu.VMEM((heads, reach + 1, rows, rows), BF),
        dma((reach, 2)), dma((reach, 2)),
        dma((rounds,)), dma((rounds,)),
        dma((rounds,)), dma((rounds,)),
        dma((rounds,)), dma((rounds,)),
        dma((max(1, head_n - 1),)), dma((max(1, head_n - 1),)),
        dma((max(1, seq_n - 1),)), dma((max(1, seq_n - 1),)),
        dma((reach, 2)), dma((reach, 2)),
    ]
    vmem = pl.BlockSpec(memory_space=pltpu.VMEM)
    results = pl.pallas_call(
        functools.partial(kernel, seq_n, head_n, reach, rounds, heads, width),
        out_shape=outs,
        in_specs=[vmem] * 9,
        out_specs=[vmem] * 9,
        scratch_shapes=scratch,
        compiler_params=pltpu.CompilerParams(
            collective_id=0, has_side_effects=True, vmem_limit_bytes=48 * 1024 * 1024
        ),
    )(
        flat(att_query), flat(att_key), flat(att_value), norm_gain, flat(dn_query), flat(dn_key),
        write_rate, log_decay, flat(out_grad),
    )

    def tall(a):
        return a.reshape(rows, heads, width)

    o, qg, kg, vg, gg, dqg, dkg, rg, cg = results
    return (tall(o), tall(qg), tall(kg), tall(vg), gg, tall(dqg), tall(dkg), rg, cg)


def solution(mesh):
    cube = P("seq", "head", None)
    pair = P("seq", "head")
    return jax.shard_map(
        body,
        mesh=mesh,
        in_specs=(cube, cube, cube, P("head", None), cube, cube, pair, pair, cube),
        out_specs=(cube, cube, cube, cube, P("head", None), cube, cube, pair, pair),
        check_vma=False,
    )
```

```python
import functools

import jax
import jax.numpy as jnp
from jax import lax
from jax.experimental import pallas as pl
from jax.experimental.pallas import tpu as pltpu
from jax.sharding import PartitionSpec as P

WIN = 1024
EPSILON = 1e-06
MESH = pl.DeviceIdType.MESH
F32 = jnp.float32
BF = jnp.bfloat16
NN = (((1,), (0,)), ((), ()))
NT = (((1,), (1,)), ((), ()))
TN = (((0,), (0,)), ((), ()))


def dot(a, b, dims=NN):
    return lax.dot_general(a.astype(BF), b.astype(BF), dims, preferred_element_type=F32)


def halves(a):
    high = a.astype(BF)
    return high, (a - high.astype(F32)).astype(BF)


def dot3(a, b, dims=NN):
    if a.dtype == BF and b.dtype == BF:
        return dot(a, b, dims)
    if a.dtype == BF:
        bh, bl = halves(b)
        return dot(a, bh, dims) + dot(a, bl, dims)
    if b.dtype == BF:
        ah, al = halves(a)
        return dot(ah, b, dims) + dot(al, b, dims)
    ah, al = halves(a)
    bh, bl = halves(b)
    return dot(ah, bh, dims) + (dot(ah, bl, dims) + dot(al, bh, dims))


def row_sum(a):
    return jnp.sum(a, axis=1, keepdims=True)


def col_sum(a):
    return jnp.sum(a, axis=0, keepdims=True)


def kernel(
    seq_n, head_n, reach, rounds, heads, width,
    q_ref, k_ref, v_ref, gain_ref, dq_ref, dk_ref, rate_ref, decay_ref, og_ref,
    out_ref, qg_ref, kg_ref, vg_ref, gg_ref, dqg_ref, dkg_ref, rg_ref, cg_ref,
    kv_in, fm_out, fm_in, fa_out, fa_in, bk_out, bk_in, hs_out, hs_in, gn_out, gn_in, gr_out, gr_in, gx_in,
    t_s, ratio_s, p_s, kkr_s, score_s, weight_s,
    kv_ss, kv_rs, fm_ss, fm_rs, fa_ss, fa_rs, bk_ss, bk_rs, hs_ss, hs_rs, gn_ss, gn_rs, gr_ss, gr_rs,
):
    rows = q_ref.shape[0]
    me = lax.axis_index("seq")
    my_head = lax.axis_index("head")
    cols = [slice(h * width, (h + 1) * width) for h in range(heads)]

    def seq_copy(src, dst, send_sem, recv_sem, shift):
        target = lax.rem(me + (shift + seq_n), seq_n)
        return pltpu.make_async_remote_copy(
            src_ref=src, dst_ref=dst, send_sem=send_sem, recv_sem=recv_sem,
            device_id={"seq": target}, device_id_type=MESH,
        )

    def head_copy(step):
        target = lax.rem(my_head + step, head_n)
        return pltpu.make_async_remote_copy(
            src_ref=hs_out, dst_ref=hs_in.at[step - 1], send_sem=hs_ss.at[step - 1],
            recv_sem=hs_rs.at[step - 1], device_id={"head": target}, device_id_type=MESH,
        )

    def kv_copies(b):
        return [
            seq_copy(ref, kv_in.at[b - 1, i], kv_ss.at[b - 1, i], kv_rs.at[b - 1, i], b)
            for i, ref in enumerate((k_ref, v_ref))
        ]

    odd = lax.rem(me, 2) == 1
    even = jnp.logical_not(odd)
    partner = me + 1 - 2 * lax.rem(me, 2)

    def partner_copy(src, dst, send_sem, recv_sem):
        return pltpu.make_async_remote_copy(
            src_ref=src, dst_ref=dst, send_sem=send_sem, recv_sem=recv_sem,
            device_id={"seq": partner}, device_id_type=MESH,
        )

    def hand_copies(b, slot):
        source = [k_ref, v_ref] if slot == 0 else [kv_in.at[slot - 1, i] for i in range(2)]
        return [
            partner_copy(source[i], kv_in.at[b - 1, i], kv_ss.at[b - 1, i], kv_rs.at[b - 1, i])
            for i in range(2)
        ]

    def cross_copies(b):
        return [
            partner_copy(gr_out.at[b - 1, i], gx_in.at[b - 1, i], gr_ss.at[b - 1, i], gr_rs.at[b - 1, i])
            for i in range(2)
        ]

    def grad_copies(b):
        return [
            seq_copy(gr_out.at[b - 1, i], gr_in.at[b - 1, i], gr_ss.at[b - 1, i], gr_rs.at[b - 1, i], -2)
            for i in range(2)
        ]

    def fm_copy(r):
        return seq_copy(fm_out.at[r], fm_in.at[r], fm_ss.at[r], fm_rs.at[r], 1 << r)

    def fa_copy(r):
        return seq_copy(fa_out.at[r], fa_in.at[r], fa_ss.at[r], fa_rs.at[r], 1 << r)

    def bk_copy(r):
        return seq_copy(bk_out.at[r], bk_in.at[r], bk_ss.at[r], bk_rs.at[r], -(1 << r))

    def gain_copy(step):
        return seq_copy(gn_out, gn_in.at[step - 1], gn_ss.at[step - 1], gn_rs.at[step - 1], step)

    def up_ok(d):
        return me + d < seq_n

    def down_ok(d):
        return me - d >= 0

    def start_if(condition, copies):
        @pl.when(condition)
        def _():
            for copy in copies:
                copy.start()

    def recv_if(condition, copies):
        @pl.when(condition)
        def _():
            for copy in copies:
                copy.wait_recv()

    def send_wait_if(condition, copies):
        @pl.when(condition)
        def _():
            for copy in copies:
                copy.wait_send()

    for b in range(1, reach + 1):
        @pl.when(jnp.logical_not(down_ok(b)))
        def _():
            kv_in[b - 1] = jnp.zeros(kv_in.shape[1:], BF)

        @pl.when(partner - b < 0)
        def _():
            gx_in[b - 1] = jnp.zeros(gx_in.shape[1:], BF)

        @pl.when(jnp.logical_not(up_ok(2)))
        def _():
            gr_in[b - 1] = jnp.zeros(gr_in.shape[1:], BF)
    for r in range(rounds):
        @pl.when(jnp.logical_not(down_ok(1 << r)))
        def _():
            fm_in[r] = jnp.zeros(fm_in.shape[1:], BF)
            fa_in[r] = jnp.zeros(fa_in.shape[1:], BF)

        @pl.when(jnp.logical_not(up_ok(1 << r)))
        def _():
            bk_in[r] = jnp.zeros(bk_in.shape[1:], BF)

    barrier = pltpu.get_barrier_semaphore()
    for step in range(1, seq_n):
        pl.semaphore_signal(barrier, inc=1, device_id={"seq": lax.rem(me + step, seq_n)}, device_id_type=MESH)
    for step in range(1, head_n):
        pl.semaphore_signal(barrier, inc=1, device_id={"head": lax.rem(my_head + step, head_n)}, device_id_type=MESH)
    pl.semaphore_wait(barrier, seq_n + head_n - 2)

    for b in range(2, reach + 1, 2):
        start_if(up_ok(b), kv_copies(b))
    start_if(even, hand_copies(1, 0))

    def hand_on(slot):
        recv_if(down_ok(slot), kv_copies(slot))
        if slot + 1 < reach:
            start_if(jnp.logical_and(even, partner - (slot + 1) >= 0), hand_copies(slot + 1, slot))
        start_if(jnp.logical_and(odd, partner - (slot - 1) >= 0), hand_copies(slot - 1, slot))

    at_row = lax.broadcasted_iota(jnp.int32, (rows, rows), 0)
    at_col = lax.broadcasted_iota(jnp.int32, (rows, rows), 1)
    lower = at_row >= at_col
    strict = at_row > at_col
    diagonal = at_row == at_col
    eye = diagonal.astype(F32)

    def to_row(column):
        return col_sum(jnp.where(diagonal, column, 0.0))

    def to_col(line):
        return row_sum(jnp.where(diagonal, line, 0.0))

    state = []
    for h in range(heads):
        xq, xk, dout = dq_ref[:, cols[h]], dk_ref[:, cols[h]], og_ref[:, cols[h]]
        fq, fk = xq.astype(F32), xk.astype(F32)
        rq = lax.rsqrt(row_sum(fq * fq) + EPSILON)
        rk = lax.rsqrt(row_sum(fk * fk) + EPSILON)
        rk_row = to_row(rk)
        rate = rate_ref[:, h : h + 1]
        decay_row = to_row(decay_ref[:, h : h + 1])
        cum = row_sum(jnp.where(lower, decay_row, 0.0))
        cum_row = to_row(cum)
        ratio = jnp.where(lower, jnp.exp(jnp.where(lower, cum - cum_row, 0.0)), 0.0)
        gamma = jnp.exp(cum)
        last = cum[rows - 1 : rows, :]
        retain = jnp.exp(last - cum)
        whole = jnp.exp(last)
        kkr = dot(xk, xk, NT) * (rk * rk_row) * ratio
        p = dot(xq, xk, NT) * (rq * rk_row) * ratio
        ratio_s[h] = ratio
        kkr_s[h] = kkr
        p_s[h] = p
        system = jnp.where(strict, rate * kkr, 0.0)
        state.append(dict(
            rq=rq, rk=rk, rate=rate, gamma=gamma, retain=retain, whole=whole,
            q=fq * rq, k=fk * rk, system=system, dout=dout,
        ))
    inverse_of = []
    for h in range(heads):
        off = ((at_row >> 1) == (at_col >> 1))
        inverse_of.append(eye - jnp.where(off, state[h]["system"], 0.0))
    level = 1
    while (1 << level) < rows:
        off = ((at_row >> (level + 1)) == (at_col >> (level + 1))) & ((at_row >> level) != (at_col >> level))
        for h in range(heads):
            x = inverse_of[h]
            y = dot3(x, jnp.where(off, state[h]["system"], 0.0))
            inverse_of[h] = x - dot3(y, x)
        level += 1
        if level == 5:
            hand_on(2)
    for slot in range(4, reach + 1, 2):
        hand_on(slot)
    for h in range(heads):
        s = state[h]
        t = inverse_of[h]
        t_s[h] = t
        kr = s["k"] * s["retain"]
        w = dot3(t, s["rate"] * s["gamma"] * s["k"])
        y = s["gamma"] * s["q"] - dot3(p_s[h], w)
        small = lax.broadcasted_iota(jnp.int32, (width, width), 0) == lax.broadcasted_iota(jnp.int32, (width, width), 1)
        diag = jnp.where(small, s["whole"], 0.0)
        s["kr"], s["w"] = kr, w
        s["fm"] = diag - dot3(kr, w, TN)
        s["bm"] = diag - dot3(w, kr, TN)
        s["bb"] = dot3(y, s["dout"], TN)
        s["em"] = s["ea"] = s["eb"] = s["ebm"] = None

    def block(h, part=0, parts=1):
        return slice((part * heads + h) * width, (part * heads + h + 1) * width)

    def forward_send(r):
        for h in range(heads):
            fm_out[r, block(h)] = state[h]["fm"].astype(BF)
        start_if(up_ok(1 << r), [fm_copy(r)])

    def back_send(r):
        for h in range(heads):
            bk_out[r, block(h)] = state[h]["bm"].astype(BF)
            bk_out[r, block(h, 1)] = state[h]["bb"].astype(BF)
        start_if(down_ok(1 << r), [bk_copy(r)])

    def back_take(r):
        recv_if(up_ok(1 << r), [bk_copy(r)])
        for h in range(heads):
            s = state[h]
            m, b = bk_in[r, block(h)], bk_in[r, block(h, 1)]
            if r == 0:
                s["ebm"], s["eb"] = m.astype(F32), b.astype(F32)
            else:
                s["eb"] = s["eb"] + dot(s["ebm"], b)
                if r < rounds - 1:
                    s["ebm"] = dot(s["ebm"], m)
            if r < rounds - 1:
                s["bb"] = s["bb"] + dot(s["bm"], b)
                s["bm"] = dot(s["bm"], m)

    def forward_take(r):
        recv_if(down_ok(1 << r), [fm_copy(r)])
        for h in range(heads):
            s = state[h]
            m = fm_in[r, block(h)]
            s.setdefault("own", []).append(s["fm"])
            if r == 0:
                s["before"] = [None, m.astype(F32)]
            else:
                s["before"].append(dot(s["before"][-1], m) if r < rounds - 1 else None)
            if r < rounds - 1:
                s["fm"] = dot(s["fm"], m)

    scale = width ** (-0.5)

    def score_block(b):
        if b % 2 == 1:
            recv_if(down_ok(b), hand_copies(b, 0))
        for h in range(heads):
            keys = k_ref[:, cols[h]] if b == 0 else kv_in[b - 1, 0, :, cols[h]]
            sc = dot(q_ref[:, cols[h]], keys, NT) * scale
            if b == 0:
                sc = jnp.where(lower, sc, -1e30)
            elif b == reach:
                sc = jnp.where(jnp.logical_and(at_col > at_row, down_ok(b)), sc, -1e30)
            else:
                sc = jnp.where(down_ok(b), sc, -1e30)
            score_s[h, b] = sc

    def attend(h):
        s = state[h]
        top = jnp.max(score_s[h, 0], axis=1, keepdims=True)
        for b in range(1, reach + 1):
            top = jnp.maximum(top, jnp.max(score_s[h, b], axis=1, keepdims=True))
        total = 0.0
        for b in range(reach + 1):
            e = jnp.exp(score_s[h, b] - top)
            score_s[h, b] = e
            total = total + row_sum(e)
        share = 1.0 / total
        attended = 0.0
        for b in range(reach + 1):
            w = score_s[h, b] * share
            score_s[h, b] = w
            wb = w.astype(BF)
            weight_s[h, b] = wb
            values = v_ref[:, cols[h]] if b == 0 else kv_in[b - 1, 1, :, cols[h]]
            attended = attended + dot(wb, values)
        s["att"] = attended

    back_send(0)
    forward_send(0)
    score_block(0)
    beside = [[2], list(range(4, reach + 1, 2)) + list(range(1, reach + 1, 2))]
    for r in range(max(rounds, 3)):
        if r < rounds:
            back_take(r)
            if r < rounds - 1:
                back_send(r + 1)
            forward_take(r)
            if r < rounds - 1:
                forward_send(r + 1)
        if r < 2:
            for b in beside[r]:
                score_block(b)
        if r == 1:
            for h in range(heads):
                attend(h)
    square = 0.0
    inner = 0.0
    for h in range(heads):
        s = state[h]
        dn = dot3(p_s[h], s["dout"], TN) + dot3(s["kr"], s["eb"])
        s["r"] = dot3(t_s[h], dn, TN)
        s["vg"] = (s["rate"] * s["r"]).astype(BF).astype(F32)
        s["weighted"] = s["vg"] * gain_ref[h : h + 1, :]
        square = square + row_sum(s["att"] * s["att"])
        inner = inner + row_sum(s["weighted"] * s["att"])
    hs_out[0:8] = jnp.broadcast_to(to_row(square), (8, rows))
    hs_out[8:16] = jnp.broadcast_to(to_row(inner), (8, rows))
    for step in range(1, head_n):
        head_copy(step).start()
    sums = hs_out[...]
    for step in range(1, head_n):
        head_copy(step).wait_recv()
        sums = sums + hs_in[step - 1]
    features = heads * head_n * width
    inverse = lax.rsqrt(to_col(sums[0:1]) / features + EPSILON)
    slope = inverse * inverse * inverse * to_col(sums[8:9]) / features
    gains = []
    for h in range(heads):
        s = state[h]
        scaled = s["att"] * inverse
        gains.append(col_sum(s["vg"] * scaled))
        s["val"] = (scaled * gain_ref[h : h + 1, :]).astype(BF)
        s["datt"] = (inverse * s["weighted"] - s["att"] * slope).astype(BF)
        s["u0"] = dot3(t_s[h], s["rate"] * s["val"].astype(F32))
        s["fa"] = dot3(s["kr"], s["u0"], TN)

    def add_send(r):
        for h in range(heads):
            fa_out[r, block(h)] = state[h]["fa"].astype(BF)
        start_if(up_ok(1 << r), [fa_copy(r)])

    def add_take(r):
        recv_if(down_ok(1 << r), [fa_copy(r)])
        for h in range(heads):
            s = state[h]
            a = fa_in[r, block(h)]
            s["ea"] = a.astype(F32) if r == 0 else s["ea"] + dot(s["before"][r], a)
            if r < rounds - 1:
                s["fa"] = s["fa"] + dot(s["own"][r], a)

    add_send(0)
    gn_out[...] = jnp.concatenate(gains + [jnp.zeros((8 - heads, width), F32)], axis=0)
    for step in range(1, seq_n):
        gain_copy(step).start()

    for h in range(heads):
        s = state[h]
        s["mean"] = row_sum(s["datt"].astype(F32) * s["att"])
        s["dqa"] = 0.0
    own_grad = []
    turn = 0
    for b in list(range(reach - 1, 0, -2)) + list(range(reach, 0, -2)) + [0]:
        for h in range(heads):
            s = state[h]
            keys = k_ref[:, cols[h]] if b == 0 else kv_in[b - 1, 0, :, cols[h]]
            values = v_ref[:, cols[h]] if b == 0 else kv_in[b - 1, 1, :, cols[h]]
            dw = dot(s["datt"], values, NT).astype(BF).astype(F32)
            ds = (score_s[h, b] * (dw - s["mean"]) * scale).astype(BF)
            s["dqa"] = s["dqa"] + dot(ds, keys)
            dkey = dot(ds, q_ref[:, cols[h]], TN)
            dval = dot(weight_s[h, b], s["datt"], TN)
            if b > 0:
                gr_out[b - 1, 0, :, cols[h]] = dkey.astype(BF)
                gr_out[b - 1, 1, :, cols[h]] = dval.astype(BF)
            else:
                own_grad.append((dkey, dval))
        if b % 2 == 1:
            start_if(down_ok(b), cross_copies(b))
        if turn < rounds:
            add_take(turn)
            if turn < rounds - 1:
                add_send(turn + 1)
        turn += 1
    for r in range(turn, rounds):
        add_take(r)
        if r < rounds - 1:
            add_send(r + 1)
    for h in range(heads):
        qg_ref[:, cols[h]] = state[h]["dqa"].astype(BF)

    def cross_add(b):
        recv_if(partner - b >= 0, cross_copies(b))
        if b > 1:
            @pl.when(jnp.logical_and(even, down_ok(b - 1)))
            def _():
                total = gr_out[b - 2].astype(F32) + gx_in[b - 1].astype(F32)
                gr_out[b - 2] = total.astype(BF)

        @pl.when(jnp.logical_and(odd, down_ok(b + 1)))
        def _():
            total = gr_out[b].astype(F32) + gx_in[b - 1].astype(F32)
            gr_out[b] = total.astype(BF)

    def finish(h):
        s = state[h]
        start, later = s["ea"], s["eb"]
        q, k, rate, gamma, retain = s["q"], s["k"], s["rate"], s["gamma"], s["retain"]
        r, dout = s["r"], s["dout"]
        fout = dout.astype(F32)
        ks = dot(k, start)
        qs = dot(q, start)
        new = s["u0"] - dot3(s["w"], start)
        p = p_s[h]
        out_ref[:, cols[h]] = (gamma * qs + dot(p, new)).astype(BF)
        dp = dot(dout, new, NT)
        da = jnp.where(strict, -dot(r, new, NT), 0.0)
        ratio, kkr = ratio_s[h], kkr_s[h]
        dqk = (dp * ratio)
        dkk = da * (rate * ratio)
        ak = da * kkr
        e = dp * p + ak * rate
        vals = s["val"].astype(F32)
        rate_grad = row_sum(ak) + row_sum(r * (vals - gamma * ks))
        down = -rate * r
        dgamma = row_sum(down * ks + fout * qs)
        dks = gamma * down
        dq = dot(gamma * fout, start, NT) + dot(dqk, k)
        dkr = dot(new, later, NT)
        dk = (
            dot(dks, start, NT) + dot(dqk, q, TN) + dot(dkk, k) + dot(dkk, k, TN) + retain * dkr
        )
        dret = row_sum(dkr * k) * retain
        dlast = col_sum(dret) + s["whole"] * col_sum(row_sum(later * start))
        dcum = to_row(row_sum(e) + dgamma * gamma - dret) - col_sum(e)
        cg_ref[:, h : h + 1] = row_sum(jnp.where(at_col >= at_row, dcum, 0.0)) + dlast
        rg_ref[:, h : h + 1] = rate_grad
        dqg_ref[:, cols[h]] = (s["rq"] * (dq - q * row_sum(q * dq))).astype(BF)
        dkg_ref[:, cols[h]] = (s["rk"] * (dk - k * row_sum(k * dk))).astype(BF)

    def chain_add(b):
        ready = jnp.logical_and(up_ok(2), me + 2 - b >= 0)
        recv_if(ready, grad_copies(b))

        @pl.when(jnp.logical_and(ready, down_ok(b - 2)))
        def _():
            total = gr_out[b - 3].astype(F32) + gr_in[b - 1].astype(F32)
            gr_out[b - 3] = total.astype(BF)

    finished = 0
    for b in range(reach - 1, 0, -2):
        cross_add(b)
        if b + 3 <= reach:
            chain_add(b + 3)
        start_if(down_ok(b + 1), grad_copies(b + 1))
        if finished < heads:
            finish(finished)
            finished += 1
    for h in range(finished, heads):
        finish(h)

    gain = gn_out[...]
    for step in range(1, seq_n):
        gain_copy(step).wait_recv()
        gain = gain + gn_in[step - 1]
    gg_ref[...] = gain[0:heads]
    recv_if(up_ok(2), grad_copies(2))
    for h in range(heads):
        dkey, dval = own_grad[h]
        dkey = dkey + jnp.where(even, gx_in[0, 0, :, cols[h]].astype(F32), 0.0)
        dval = dval + jnp.where(even, gx_in[0, 1, :, cols[h]].astype(F32), 0.0)
        dkey = dkey + gr_in[1, 0, :, cols[h]].astype(F32)
        dval = dval + gr_in[1, 1, :, cols[h]].astype(F32)
        kg_ref[:, cols[h]] = dkey.astype(BF)
        vg_ref[:, cols[h]] = dval.astype(BF)

    for b in range(2, reach + 1, 2):
        send_wait_if(up_ok(b), kv_copies(b))
        send_wait_if(down_ok(b), grad_copies(b))
    for b in range(1, reach + 1, 2):
        send_wait_if(partner - b >= 0, hand_copies(b, 0))
        send_wait_if(down_ok(b), cross_copies(b))
    for r in range(rounds):
        send_wait_if(up_ok(1 << r), [fm_copy(r), fa_copy(r)])
        send_wait_if(down_ok(1 << r), [bk_copy(r)])
    for step in range(1, head_n):
        head_copy(step).wait_send()
    for step in range(1, seq_n):
        gain_copy(step).wait_send()


def body(att_query, att_key, att_value, norm_gain, dn_query, dn_key, write_rate, log_decay, out_grad):
    rows, heads, width = att_query.shape
    seq_n, head_n = lax.axis_size("seq"), lax.axis_size("head")
    reach = max(1, WIN // rows)
    rounds = max(1, (seq_n - 1).bit_length())
    wide = heads * width

    def flat(a):
        return a.reshape(rows, wide)

    big = jax.ShapeDtypeStruct((rows, wide), BF)
    thin = jax.ShapeDtypeStruct((rows, heads), F32)
    outs = [big, big, big, big, jax.ShapeDtypeStruct((heads, width), F32), big, big, thin, thin]
    dma = pltpu.SemaphoreType.DMA
    scratch = [
        pltpu.VMEM((reach, 2, rows, wide), BF),
        pltpu.VMEM((rounds, wide, width), BF),
        pltpu.VMEM((rounds, wide, width), BF),
        pltpu.VMEM((rounds, wide, width), BF),
        pltpu.VMEM((rounds, wide, width), BF),
        pltpu.VMEM((rounds, 2 * wide, width), BF),
        pltpu.VMEM((rounds, 2 * wide, width), BF),
        pltpu.VMEM((16, rows), F32),
        pltpu.VMEM((max(1, head_n - 1), 16, rows), F32),
        pltpu.VMEM((8, width), F32),
        pltpu.VMEM((max(1, seq_n - 1), 8, width), F32),
        pltpu.VMEM((reach, 2, rows, wide), BF),
        pltpu.VMEM((reach, 2, rows, wide), BF),
        pltpu.VMEM((reach, 2, rows, wide), BF),
        pltpu.VMEM((heads, rows, rows), F32),
        pltpu.VMEM((heads, rows, rows), F32),
        pltpu.VMEM((heads, rows, rows), F32),
        pltpu.VMEM((heads, rows, rows), F32),
        pltpu.VMEM((heads, reach + 1, rows, rows), F32),
        pltpu.VMEM((heads, reach + 1, rows, rows), BF),
        dma((reach, 2)), dma((reach, 2)),
        dma((rounds,)), dma((rounds,)),
        dma((rounds,)), dma((rounds,)),
        dma((rounds,)), dma((rounds,)),
        dma((max(1, head_n - 1),)), dma((max(1, head_n - 1),)),
        dma((max(1, seq_n - 1),)), dma((max(1, seq_n - 1),)),
        dma((reach, 2)), dma((reach, 2)),
    ]
    vmem = pl.BlockSpec(memory_space=pltpu.VMEM)
    results = pl.pallas_call(
        functools.partial(kernel, seq_n, head_n, reach, rounds, heads, width),
        out_shape=outs,
        in_specs=[vmem] * 9,
        out_specs=[vmem] * 9,
        scratch_shapes=scratch,
        compiler_params=pltpu.CompilerParams(
            collective_id=0, has_side_effects=True, vmem_limit_bytes=48 * 1024 * 1024
        ),
    )(
        flat(att_query), flat(att_key), flat(att_value), norm_gain, flat(dn_query), flat(dn_key),
        write_rate, log_decay, flat(out_grad),
    )

    def tall(a):
        return a.reshape(rows, heads, width)

    o, qg, kg, vg, gg, dqg, dkg, rg, cg = results
    return (tall(o), tall(qg), tall(kg), tall(vg), gg, tall(dqg), tall(dkg), rg, cg)


def solution(mesh):
    cube = P("seq", "head", None)
    pair = P("seq", "head")
    return jax.shard_map(
        body,
        mesh=mesh,
        in_specs=(cube, cube, cube, P("head", None), cube, cube, pair, pair, cube),
        out_specs=(cube, cube, cube, cube, P("head", None), cube, cube, pair, pair),
        check_vma=False,
    )
```

```python
import functools

import jax
import jax.numpy as jnp
from jax import lax
from jax.experimental import pallas as pl
from jax.experimental.pallas import tpu as pltpu
from jax.sharding import PartitionSpec as P

WIN = 1024
EPSILON = 1e-06
MESH = pl.DeviceIdType.MESH
F32 = jnp.float32
BF = jnp.bfloat16
NN = (((1,), (0,)), ((), ()))
NT = (((1,), (1,)), ((), ()))
TN = (((0,), (0,)), ((), ()))


def dot(a, b, dims=NN):
    return lax.dot_general(a.astype(BF), b.astype(BF), dims, preferred_element_type=F32)


def halves(a):
    high = a.astype(BF)
    return high, (a - high.astype(F32)).astype(BF)


def dot3(a, b, dims=NN):
    if a.dtype == BF and b.dtype == BF:
        return dot(a, b, dims)
    if a.dtype == BF:
        bh, bl = halves(b)
        return dot(a, bh, dims) + dot(a, bl, dims)
    if b.dtype == BF:
        ah, al = halves(a)
        return dot(ah, b, dims) + dot(al, b, dims)
    ah, al = halves(a)
    bh, bl = halves(b)
    return dot(ah, bh, dims) + (dot(ah, bl, dims) + dot(al, bh, dims))


def row_sum(a):
    return jnp.sum(a, axis=1, keepdims=True)


def col_sum(a):
    return jnp.sum(a, axis=0, keepdims=True)


def kernel(
    seq_n, head_n, reach, rounds, heads, width,
    q_ref, k_ref, v_ref, gain_ref, dq_ref, dk_ref, rate_ref, decay_ref, og_ref,
    out_ref, qg_ref, kg_ref, vg_ref, gg_ref, dqg_ref, dkg_ref, rg_ref, cg_ref,
    kv_in, fm_out, fm_in, fa_out, fa_in, bk_out, bk_in, hs_out, hs_in, gn_out, gn_in, gr_out, gr_in, gx_in,
    t_s, ratio_s, p_s, kkr_s, score_s, weight_s,
    kv_ss, kv_rs, fm_ss, fm_rs, fa_ss, fa_rs, bk_ss, bk_rs, hs_ss, hs_rs, gn_ss, gn_rs, gr_ss, gr_rs,
):
    rows = q_ref.shape[0]
    me = lax.axis_index("seq")
    my_head = lax.axis_index("head")
    cols = [slice(h * width, (h + 1) * width) for h in range(heads)]

    def seq_copy(src, dst, send_sem, recv_sem, shift):
        target = lax.rem(me + (shift + seq_n), seq_n)
        return pltpu.make_async_remote_copy(
            src_ref=src, dst_ref=dst, send_sem=send_sem, recv_sem=recv_sem,
            device_id={"seq": target}, device_id_type=MESH,
        )

    def head_copy(step):
        target = lax.rem(my_head + step, head_n)
        return pltpu.make_async_remote_copy(
            src_ref=hs_out, dst_ref=hs_in.at[step - 1], send_sem=hs_ss.at[step - 1],
            recv_sem=hs_rs.at[step - 1], device_id={"head": target}, device_id_type=MESH,
        )

    def kv_copies(b):
        return [
            seq_copy(ref, kv_in.at[b - 1, i], kv_ss.at[b - 1, i], kv_rs.at[b - 1, i], b)
            for i, ref in enumerate((k_ref, v_ref))
        ]

    odd = lax.rem(me, 2) == 1
    even = jnp.logical_not(odd)
    partner = me + 1 - 2 * lax.rem(me, 2)

    def partner_copy(src, dst, send_sem, recv_sem):
        return pltpu.make_async_remote_copy(
            src_ref=src, dst_ref=dst, send_sem=send_sem, recv_sem=recv_sem,
            device_id={"seq": partner}, device_id_type=MESH,
        )

    def hand_copies(b, slot):
        source = [k_ref, v_ref] if slot == 0 else [kv_in.at[slot - 1, i] for i in range(2)]
        return [
            partner_copy(source[i], kv_in.at[b - 1, i], kv_ss.at[b - 1, i], kv_rs.at[b - 1, i])
            for i in range(2)
        ]

    def cross_copies(b):
        return [
            partner_copy(gr_out.at[b - 1, i], gx_in.at[b - 1, i], gr_ss.at[b - 1, i], gr_rs.at[b - 1, i])
            for i in range(2)
        ]

    def grad_copies(b):
        return [
            seq_copy(gr_out.at[b - 1, i], gr_in.at[b - 1, i], gr_ss.at[b - 1, i], gr_rs.at[b - 1, i], -2)
            for i in range(2)
        ]

    def fm_copy(r):
        return seq_copy(fm_out.at[r], fm_in.at[r], fm_ss.at[r], fm_rs.at[r], 1 << r)

    def fa_copy(r):
        return seq_copy(fa_out.at[r], fa_in.at[r], fa_ss.at[r], fa_rs.at[r], 1 << r)

    def bk_copy(r):
        return seq_copy(bk_out.at[r], bk_in.at[r], bk_ss.at[r], bk_rs.at[r], -(1 << r))

    def gain_copy(step):
        return seq_copy(gn_out, gn_in.at[step - 1], gn_ss.at[step - 1], gn_rs.at[step - 1], step)

    def up_ok(d):
        return me + d < seq_n

    def down_ok(d):
        return me - d >= 0

    def start_if(condition, copies):
        @pl.when(condition)
        def _():
            for copy in copies:
                copy.start()

    def recv_if(condition, copies):
        @pl.when(condition)
        def _():
            for copy in copies:
                copy.wait_recv()

    def send_wait_if(condition, copies):
        @pl.when(condition)
        def _():
            for copy in copies:
                copy.wait_send()

    for b in range(1, reach + 1):
        @pl.when(jnp.logical_not(down_ok(b)))
        def _():
            kv_in[b - 1] = jnp.zeros(kv_in.shape[1:], BF)

        @pl.when(partner - b < 0)
        def _():
            gx_in[b - 1] = jnp.zeros(gx_in.shape[1:], BF)

        @pl.when(jnp.logical_not(up_ok(2)))
        def _():
            gr_in[b - 1] = jnp.zeros(gr_in.shape[1:], BF)
    for r in range(rounds):
        @pl.when(jnp.logical_not(down_ok(1 << r)))
        def _():
            fm_in[r] = jnp.zeros(fm_in.shape[1:], BF)
            fa_in[r] = jnp.zeros(fa_in.shape[1:], BF)

        @pl.when(jnp.logical_not(up_ok(1 << r)))
        def _():
            bk_in[r] = jnp.zeros(bk_in.shape[1:], BF)

    barrier = pltpu.get_barrier_semaphore()
    for step in range(1, seq_n):
        pl.semaphore_signal(barrier, inc=1, device_id={"seq": lax.rem(me + step, seq_n)}, device_id_type=MESH)
    for step in range(1, head_n):
        pl.semaphore_signal(barrier, inc=1, device_id={"head": lax.rem(my_head + step, head_n)}, device_id_type=MESH)
    pl.semaphore_wait(barrier, seq_n + head_n - 2)

    for b in range(2, reach + 1, 2):
        start_if(up_ok(b), kv_copies(b))
    start_if(even, hand_copies(1, 0))

    def hand_on(slot):
        recv_if(down_ok(slot), kv_copies(slot))
        if slot + 1 < reach:
            start_if(jnp.logical_and(even, partner - (slot + 1) >= 0), hand_copies(slot + 1, slot))
        start_if(jnp.logical_and(odd, partner - (slot - 1) >= 0), hand_copies(slot - 1, slot))

    at_row = lax.broadcasted_iota(jnp.int32, (rows, rows), 0)
    at_col = lax.broadcasted_iota(jnp.int32, (rows, rows), 1)
    lower = at_row >= at_col
    strict = at_row > at_col
    diagonal = at_row == at_col
    eye = diagonal.astype(F32)

    def to_row(column):
        return col_sum(jnp.where(diagonal, column, 0.0))

    def to_col(line):
        return row_sum(jnp.where(diagonal, line, 0.0))

    state = []
    for h in range(heads):
        xq, xk, dout = dq_ref[:, cols[h]], dk_ref[:, cols[h]], og_ref[:, cols[h]]
        fq, fk = xq.astype(F32), xk.astype(F32)
        rq = lax.rsqrt(row_sum(fq * fq) + EPSILON)
        rk = lax.rsqrt(row_sum(fk * fk) + EPSILON)
        rk_row = to_row(rk)
        rate = rate_ref[:, h : h + 1]
        decay_row = to_row(decay_ref[:, h : h + 1])
        cum = row_sum(jnp.where(lower, decay_row, 0.0))
        cum_row = to_row(cum)
        ratio = jnp.where(lower, jnp.exp(jnp.where(lower, cum - cum_row, 0.0)), 0.0)
        gamma = jnp.exp(cum)
        last = cum[rows - 1 : rows, :]
        retain = jnp.exp(last - cum)
        whole = jnp.exp(last)
        kkr = dot(xk, xk, NT) * (rk * rk_row) * ratio
        p = dot(xq, xk, NT) * (rq * rk_row) * ratio
        ratio_s[h] = ratio
        kkr_s[h] = kkr
        p_s[h] = p
        system = jnp.where(strict, rate * kkr, 0.0)
        state.append(dict(
            rq=rq, rk=rk, rate=rate, gamma=gamma, retain=retain, whole=whole,
            q=fq * rq, k=fk * rk, system=system, dout=dout,
        ))
    inverse_of = []
    for h in range(heads):
        off = ((at_row >> 1) == (at_col >> 1))
        inverse_of.append(eye - jnp.where(off, state[h]["system"], 0.0))
    system_halves = [halves(state[h]["system"]) for h in range(heads)]
    level = 1
    while (1 << level) < rows:
        off = ((at_row >> (level + 1)) == (at_col >> (level + 1))) & ((at_row >> level) != (at_col >> level))
        keep = jnp.where(off, 1.0, 0.0).astype(BF)
        for h in range(heads):
            x = inverse_of[h]
            xh, xl = halves(x)
            sh, sl = (half * keep for half in system_halves[h])
            yh, yl = halves(dot(xh, sh) + (dot(xh, sl) + dot(xl, sh)))
            inverse_of[h] = x - (dot(yh, xh) + (dot(yh, xl) + dot(yl, xh)))
        level += 1
        if level == 5:
            hand_on(2)
    for slot in range(4, reach + 1, 2):
        hand_on(slot)
    for h in range(heads):
        s = state[h]
        t = inverse_of[h]
        t_s[h] = t
        kr = s["k"] * s["retain"]
        w = dot3(t, s["rate"] * s["gamma"] * s["k"])
        y = s["gamma"] * s["q"] - dot3(p_s[h], w)
        small = lax.broadcasted_iota(jnp.int32, (width, width), 0) == lax.broadcasted_iota(jnp.int32, (width, width), 1)
        diag = jnp.where(small, s["whole"], 0.0)
        s["kr"], s["w"] = kr, w
        s["fm"] = diag - dot3(kr, w, TN)
        s["bm"] = diag - dot3(w, kr, TN)
        s["bb"] = dot3(y, s["dout"], TN)
        s["em"] = s["ea"] = s["eb"] = s["ebm"] = None

    def block(h, part=0, parts=1):
        return slice((part * heads + h) * width, (part * heads + h + 1) * width)

    def forward_send(r):
        for h in range(heads):
            fm_out[r, block(h)] = state[h]["fm"].astype(BF)
        start_if(up_ok(1 << r), [fm_copy(r)])

    def back_send(r):
        for h in range(heads):
            bk_out[r, block(h)] = state[h]["bm"].astype(BF)
            bk_out[r, block(h, 1)] = state[h]["bb"].astype(BF)
        start_if(down_ok(1 << r), [bk_copy(r)])

    def back_take(r):
        recv_if(up_ok(1 << r), [bk_copy(r)])
        for h in range(heads):
            s = state[h]
            m, b = bk_in[r, block(h)], bk_in[r, block(h, 1)]
            if r == 0:
                s["ebm"], s["eb"] = m.astype(F32), b.astype(F32)
            else:
                s["eb"] = s["eb"] + dot(s["ebm"], b)
                if r < rounds - 1:
                    s["ebm"] = dot(s["ebm"], m)
            if r < rounds - 1:
                s["bb"] = s["bb"] + dot(s["bm"], b)
                s["bm"] = dot(s["bm"], m)

    def forward_take(r):
        recv_if(down_ok(1 << r), [fm_copy(r)])
        for h in range(heads):
            s = state[h]
            m = fm_in[r, block(h)]
            s.setdefault("own", []).append(s["fm"])
            if r == 0:
                s["before"] = [None, m.astype(F32)]
            else:
                s["before"].append(dot(s["before"][-1], m) if r < rounds - 1 else None)
            if r < rounds - 1:
                s["fm"] = dot(s["fm"], m)

    scale = width ** (-0.5)

    def score_block(b):
        if b % 2 == 1:
            recv_if(down_ok(b), hand_copies(b, 0))
        for h in range(heads):
            keys = k_ref[:, cols[h]] if b == 0 else kv_in[b - 1, 0, :, cols[h]]
            sc = dot(q_ref[:, cols[h]], keys, NT) * scale
            if b == 0:
                sc = jnp.where(lower, sc, -1e30)
            elif b == reach:
                sc = jnp.where(jnp.logical_and(at_col > at_row, down_ok(b)), sc, -1e30)
            else:
                sc = jnp.where(down_ok(b), sc, -1e30)
            score_s[h, b] = sc

    def attend(h):
        s = state[h]
        top = jnp.max(score_s[h, 0], axis=1, keepdims=True)
        for b in range(1, reach + 1):
            top = jnp.maximum(top, jnp.max(score_s[h, b], axis=1, keepdims=True))
        total = 0.0
        for b in range(reach + 1):
            e = jnp.exp(score_s[h, b] - top)
            score_s[h, b] = e
            total = total + row_sum(e)
        share = 1.0 / total
        attended = 0.0
        for b in range(reach + 1):
            w = score_s[h, b] * share
            score_s[h, b] = w
            wb = w.astype(BF)
            weight_s[h, b] = wb
            values = v_ref[:, cols[h]] if b == 0 else kv_in[b - 1, 1, :, cols[h]]
            attended = attended + dot(wb, values)
        s["att"] = attended

    back_send(0)
    forward_send(0)
    score_block(0)
    beside = [[2], list(range(4, reach + 1, 2)) + list(range(1, reach + 1, 2))]
    for r in range(max(rounds, 3)):
        if r < rounds:
            back_take(r)
            if r < rounds - 1:
                back_send(r + 1)
            forward_take(r)
            if r < rounds - 1:
                forward_send(r + 1)
        if r < 2:
            for b in beside[r]:
                score_block(b)
        if r == 1:
            for h in range(heads):
                attend(h)
    square = 0.0
    inner = 0.0
    for h in range(heads):
        s = state[h]
        dn = dot3(p_s[h], s["dout"], TN) + dot3(s["kr"], s["eb"])
        s["r"] = dot3(t_s[h], dn, TN)
        s["vg"] = (s["rate"] * s["r"]).astype(BF).astype(F32)
        s["weighted"] = s["vg"] * gain_ref[h : h + 1, :]
        square = square + row_sum(s["att"] * s["att"])
        inner = inner + row_sum(s["weighted"] * s["att"])
    hs_out[0:8] = jnp.broadcast_to(to_row(square), (8, rows))
    hs_out[8:16] = jnp.broadcast_to(to_row(inner), (8, rows))
    for step in range(1, head_n):
        head_copy(step).start()
    sums = hs_out[...]
    for step in range(1, head_n):
        head_copy(step).wait_recv()
        sums = sums + hs_in[step - 1]
    features = heads * head_n * width
    inverse = lax.rsqrt(to_col(sums[0:1]) / features + EPSILON)
    slope = inverse * inverse * inverse * to_col(sums[8:9]) / features
    gains = []
    for h in range(heads):
        s = state[h]
        scaled = s["att"] * inverse
        gains.append(col_sum(s["vg"] * scaled))
        s["val"] = (scaled * gain_ref[h : h + 1, :]).astype(BF)
        s["datt"] = (inverse * s["weighted"] - s["att"] * slope).astype(BF)
        s["u0"] = dot3(t_s[h], s["rate"] * s["val"].astype(F32))
        s["fa"] = dot3(s["kr"], s["u0"], TN)

    def add_send(r):
        for h in range(heads):
            fa_out[r, block(h)] = state[h]["fa"].astype(BF)
        start_if(up_ok(1 << r), [fa_copy(r)])

    def add_take(r):
        recv_if(down_ok(1 << r), [fa_copy(r)])
        for h in range(heads):
            s = state[h]
            a = fa_in[r, block(h)]
            s["ea"] = a.astype(F32) if r == 0 else s["ea"] + dot(s["before"][r], a)
            if r < rounds - 1:
                s["fa"] = s["fa"] + dot(s["own"][r], a)

    add_send(0)
    gn_out[...] = jnp.concatenate(gains + [jnp.zeros((8 - heads, width), F32)], axis=0)
    for step in range(1, seq_n):
        gain_copy(step).start()

    for h in range(heads):
        s = state[h]
        s["mean"] = row_sum(s["datt"].astype(F32) * s["att"])
        s["dqa"] = 0.0
    own_grad = []
    turn = 0
    for b in list(range(reach - 1, 0, -2)) + list(range(reach, 0, -2)) + [0]:
        for h in range(heads):
            s = state[h]
            keys = k_ref[:, cols[h]] if b == 0 else kv_in[b - 1, 0, :, cols[h]]
            values = v_ref[:, cols[h]] if b == 0 else kv_in[b - 1, 1, :, cols[h]]
            dw = dot(s["datt"], values, NT).astype(BF).astype(F32)
            ds = (score_s[h, b] * (dw - s["mean"]) * scale).astype(BF)
            s["dqa"] = s["dqa"] + dot(ds, keys)
            dkey = dot(ds, q_ref[:, cols[h]], TN)
            dval = dot(weight_s[h, b], s["datt"], TN)
            if b > 0:
                gr_out[b - 1, 0, :, cols[h]] = dkey.astype(BF)
                gr_out[b - 1, 1, :, cols[h]] = dval.astype(BF)
            else:
                own_grad.append((dkey, dval))
        if b % 2 == 1:
            start_if(down_ok(b), cross_copies(b))
        if turn < rounds:
            add_take(turn)
            if turn < rounds - 1:
                add_send(turn + 1)
        turn += 1
    for r in range(turn, rounds):
        add_take(r)
        if r < rounds - 1:
            add_send(r + 1)
    for h in range(heads):
        qg_ref[:, cols[h]] = state[h]["dqa"].astype(BF)

    def cross_add(b):
        recv_if(partner - b >= 0, cross_copies(b))
        if b > 1:
            @pl.when(jnp.logical_and(even, down_ok(b - 1)))
            def _():
                total = gr_out[b - 2].astype(F32) + gx_in[b - 1].astype(F32)
                gr_out[b - 2] = total.astype(BF)

        @pl.when(jnp.logical_and(odd, down_ok(b + 1)))
        def _():
            total = gr_out[b].astype(F32) + gx_in[b - 1].astype(F32)
            gr_out[b] = total.astype(BF)

    def finish(h):
        s = state[h]
        start, later = s["ea"], s["eb"]
        q, k, rate, gamma, retain = s["q"], s["k"], s["rate"], s["gamma"], s["retain"]
        r, dout = s["r"], s["dout"]
        fout = dout.astype(F32)
        ks = dot(k, start)
        qs = dot(q, start)
        new = s["u0"] - dot3(s["w"], start)
        p = p_s[h]
        out_ref[:, cols[h]] = (gamma * qs + dot(p, new)).astype(BF)
        dp = dot(dout, new, NT)
        da = jnp.where(strict, -dot(r, new, NT), 0.0)
        ratio, kkr = ratio_s[h], kkr_s[h]
        dqk = (dp * ratio)
        dkk = da * (rate * ratio)
        ak = da * kkr
        e = dp * p + ak * rate
        vals = s["val"].astype(F32)
        rate_grad = row_sum(ak) + row_sum(r * (vals - gamma * ks))
        down = -rate * r
        dgamma = row_sum(down * ks + fout * qs)
        dks = gamma * down
        dq = dot(gamma * fout, start, NT) + dot(dqk, k)
        dkr = dot(new, later, NT)
        dk = (
            dot(dks, start, NT) + dot(dqk, q, TN) + dot(dkk, k) + dot(dkk, k, TN) + retain * dkr
        )
        dret = row_sum(dkr * k) * retain
        dlast = col_sum(dret) + s["whole"] * col_sum(row_sum(later * start))
        dcum = to_row(row_sum(e) + dgamma * gamma - dret) - col_sum(e)
        cg_ref[:, h : h + 1] = row_sum(jnp.where(at_col >= at_row, dcum, 0.0)) + dlast
        rg_ref[:, h : h + 1] = rate_grad
        dqg_ref[:, cols[h]] = (s["rq"] * (dq - q * row_sum(q * dq))).astype(BF)
        dkg_ref[:, cols[h]] = (s["rk"] * (dk - k * row_sum(k * dk))).astype(BF)

    def chain_add(b):
        ready = jnp.logical_and(up_ok(2), me + 2 - b >= 0)
        recv_if(ready, grad_copies(b))

        @pl.when(jnp.logical_and(ready, down_ok(b - 2)))
        def _():
            total = gr_out[b - 3].astype(F32) + gr_in[b - 1].astype(F32)
            gr_out[b - 3] = total.astype(BF)

    finished = 0
    for b in range(reach - 1, 0, -2):
        cross_add(b)
        if b + 3 <= reach:
            chain_add(b + 3)
        start_if(down_ok(b + 1), grad_copies(b + 1))
        if finished < heads:
            finish(finished)
            finished += 1
    for h in range(finished, heads):
        finish(h)

    gain = gn_out[...]
    for step in range(1, seq_n):
        gain_copy(step).wait_recv()
        gain = gain + gn_in[step - 1]
    gg_ref[...] = gain[0:heads]
    recv_if(up_ok(2), grad_copies(2))
    for h in range(heads):
        dkey, dval = own_grad[h]
        dkey = dkey + jnp.where(even, gx_in[0, 0, :, cols[h]].astype(F32), 0.0)
        dval = dval + jnp.where(even, gx_in[0, 1, :, cols[h]].astype(F32), 0.0)
        dkey = dkey + gr_in[1, 0, :, cols[h]].astype(F32)
        dval = dval + gr_in[1, 1, :, cols[h]].astype(F32)
        kg_ref[:, cols[h]] = dkey.astype(BF)
        vg_ref[:, cols[h]] = dval.astype(BF)

    for b in range(2, reach + 1, 2):
        send_wait_if(up_ok(b), kv_copies(b))
        send_wait_if(down_ok(b), grad_copies(b))
    for b in range(1, reach + 1, 2):
        send_wait_if(partner - b >= 0, hand_copies(b, 0))
        send_wait_if(down_ok(b), cross_copies(b))
    for r in range(rounds):
        send_wait_if(up_ok(1 << r), [fm_copy(r), fa_copy(r)])
        send_wait_if(down_ok(1 << r), [bk_copy(r)])
    for step in range(1, head_n):
        head_copy(step).wait_send()
    for step in range(1, seq_n):
        gain_copy(step).wait_send()


def body(att_query, att_key, att_value, norm_gain, dn_query, dn_key, write_rate, log_decay, out_grad):
    rows, heads, width = att_query.shape
    seq_n, head_n = lax.axis_size("seq"), lax.axis_size("head")
    reach = max(1, WIN // rows)
    rounds = max(1, (seq_n - 1).bit_length())
    wide = heads * width

    def flat(a):
        return a.reshape(rows, wide)

    big = jax.ShapeDtypeStruct((rows, wide), BF)
    thin = jax.ShapeDtypeStruct((rows, heads), F32)
    outs = [big, big, big, big, jax.ShapeDtypeStruct((heads, width), F32), big, big, thin, thin]
    dma = pltpu.SemaphoreType.DMA
    scratch = [
        pltpu.VMEM((reach, 2, rows, wide), BF),
        pltpu.VMEM((rounds, wide, width), BF),
        pltpu.VMEM((rounds, wide, width), BF),
        pltpu.VMEM((rounds, wide, width), BF),
        pltpu.VMEM((rounds, wide, width), BF),
        pltpu.VMEM((rounds, 2 * wide, width), BF),
        pltpu.VMEM((rounds, 2 * wide, width), BF),
        pltpu.VMEM((16, rows), F32),
        pltpu.VMEM((max(1, head_n - 1), 16, rows), F32),
        pltpu.VMEM((8, width), F32),
        pltpu.VMEM((max(1, seq_n - 1), 8, width), F32),
        pltpu.VMEM((reach, 2, rows, wide), BF),
        pltpu.VMEM((reach, 2, rows, wide), BF),
        pltpu.VMEM((reach, 2, rows, wide), BF),
        pltpu.VMEM((heads, rows, rows), F32),
        pltpu.VMEM((heads, rows, rows), F32),
        pltpu.VMEM((heads, rows, rows), F32),
        pltpu.VMEM((heads, rows, rows), F32),
        pltpu.VMEM((heads, reach + 1, rows, rows), F32),
        pltpu.VMEM((heads, reach + 1, rows, rows), BF),
        dma((reach, 2)), dma((reach, 2)),
        dma((rounds,)), dma((rounds,)),
        dma((rounds,)), dma((rounds,)),
        dma((rounds,)), dma((rounds,)),
        dma((max(1, head_n - 1),)), dma((max(1, head_n - 1),)),
        dma((max(1, seq_n - 1),)), dma((max(1, seq_n - 1),)),
        dma((reach, 2)), dma((reach, 2)),
    ]
    vmem = pl.BlockSpec(memory_space=pltpu.VMEM)
    results = pl.pallas_call(
        functools.partial(kernel, seq_n, head_n, reach, rounds, heads, width),
        out_shape=outs,
        in_specs=[vmem] * 9,
        out_specs=[vmem] * 9,
        scratch_shapes=scratch,
        compiler_params=pltpu.CompilerParams(
            collective_id=0, has_side_effects=True, vmem_limit_bytes=48 * 1024 * 1024
        ),
    )(
        flat(att_query), flat(att_key), flat(att_value), norm_gain, flat(dn_query), flat(dn_key),
        write_rate, log_decay, flat(out_grad),
    )

    def tall(a):
        return a.reshape(rows, heads, width)

    o, qg, kg, vg, gg, dqg, dkg, rg, cg = results
    return (tall(o), tall(qg), tall(kg), tall(vg), gg, tall(dqg), tall(dkg), rg, cg)


def solution(mesh):
    cube = P("seq", "head", None)
    pair = P("seq", "head")
    return jax.shard_map(
        body,
        mesh=mesh,
        in_specs=(cube, cube, cube, P("head", None), cube, cube, pair, pair, cube),
        out_specs=(cube, cube, cube, cube, P("head", None), cube, cube, pair, pair),
        check_vma=False,
    )
```
